32 devices in a mesh: section: 4 (over z), tensor: 2 (over x), dp: 4 (over y, core).
Axes of the slice: x: 2, y: 2, z: 4, core: 2. Of those that a mesh axis runs over, the one named last changes fastest.
Arguments:
- parked: bfloat16 [4, 2, 128, 6144], P('section', None, 'tensor', 'dp'), may hold values from -6 to 6
- arriving: bfloat16 [4, 128, 6144], P('section', 'tensor', 'dp'), may hold values from -6 to 6
- slot_table: int32 [4, 2], replicated, may hold values from 0 to 1, each once within a row
- value_weight: bfloat16 [4, 6144, 8192], P('section', 'dp', 'tensor'), may hold values from -0.078125 to 0.078125
- output_weight: bfloat16 [4, 8192, 6144], P('section', 'tensor', 'dp'), may hold values from -0.0625 to 0.0625
- slopes: float32 [64], P('tensor'), may hold values from 0.004 to 0.12
Outputs:
- sent: bfloat16 [4, 128, 6144], P('section', 'tensor', 'dp')
- value_grad: bfloat16 [4, 6144, 8192], P('section', 'dp', 'tensor')
The draws below stay inside these ranges and needn't reach their ends.
Inputs may be any that keep to these rules, and one draw needn't show every extreme that they name: `slot_table`: each row is a permutation of 0 to 1.
All inputs are finite; a program needn't handle non-finite values.
Results may differ from the reference program's by a relative error of at most 0.0065.
The reference program's roundings to bfloat16 on the way (of `mixing`, `inputs`, `upstream`, `normed`, `grad_mixed`, `grad_value` and `grad_input`) count: a program that leaves them out, or rounds other values in their place, can miss the bound.
Values may be sent and summed in bfloat16 or wider, within the bound.
No kernel may reach another device: no remote copies, remote signals or barrier semaphores. Data moves between devices by JAX's collectives and lax.ppermute only.
A program may use at most 192 MiB of HBM per device.

```python
import math
import jax
import jax.numpy as jnp
from jax import lax

D = 6144
HEADS = 64
SLOTS = 2
F = 8192
LEN = 128
SECTIONS = 4


def block_levels(rng, extent, split, low, top_value):
    loudness, own = 1.0, jax.random.fold_in(rng, 6)
    for position, blocks in split:
        draws = jnp.exp(jax.random.uniform(jax.random.fold_in(own, position), (blocks,), jnp.float32, low / len(split), top_value / len(split)))
        loudness = loudness * jnp.repeat(draws, extent[position] // blocks).reshape([-1 if axis == position else 1 for axis in range(len(extent))])
    return loudness


def bell_draw(rng, dims, scale, reach, shards=(), dtype=jnp.bfloat16):
    values = jax.random.normal(rng, dims, jnp.float32) * scale
    if len(shards) > 0:
        values = block_levels(rng, dims, shards, -0.22, 0.18) * values
    return jnp.clip(values, min=-reach, max=reach).astype(dtype)


def setup_inputs(seed: int = 0) -> dict:
    keys = jax.random.split(jax.random.key(seed), 7)
    return {
        "parked": bell_draw(keys[0], (SECTIONS, SLOTS, LEN, D), 1.0, 6.0, ((0, 4), (2, 2), (3, 4))),
        "arriving": bell_draw(keys[1], (SECTIONS, LEN, D), 1.0, 6.0, ((0, 4), (1, 2), (2, 4))),
        "slot_table": jax.vmap(lambda own: jax.random.permutation(own, SLOTS))(jax.random.split(keys[2], SECTIONS)).reshape((SECTIONS, SLOTS)).astype(jnp.int32),
        "value_weight": bell_draw(keys[3], (SECTIONS, D, F), D ** -0.5, 0.078125, ((0, 4), (1, 4), (2, 2))),
        "output_weight": bell_draw(keys[4], (SECTIONS, F, D), F ** -0.5, 0.0625, ((0, 4), (1, 2), (2, 4))),
        "slopes": jnp.clip(jnp.exp(math.log(0.12) - 3.4011973 * jax.random.uniform(keys[5], (HEADS,), jnp.float32) ** block_levels(keys[5], (HEADS,), ((0, 2),), -0.2, 0.2)), 0.004, 0.12),
    }


EPSILON = 1e-05

def mixing_weights(slopes, length):
    places = jnp.arange(length)
    distance = (places[:, None] - places[None, :]).astype(jnp.float32)
    causal = distance >= 0
    logits = -slopes[:, None, None] * jnp.where(causal, distance, 0.0)[None, :, :]
    weights = jnp.where(causal[None, :, :], jnp.exp(logits), 0.0)
    return (weights / lax.optimization_barrier(jnp.sum(weights, axis=-1, keepdims=True))).astype(jnp.bfloat16)

def layer_step(inputs, upstream, w_value, w_output, mixing):
    length = inputs.shape[0]
    heads_count = mixing.shape[0]
    floats = inputs.astype(jnp.float32)
    center = lax.optimization_barrier(jnp.mean(floats, axis=-1, keepdims=True))
    spread = lax.optimization_barrier(jnp.mean(floats * floats, axis=-1, keepdims=True)) - center * center
    inverse = lax.rsqrt(spread + EPSILON)
    scaled = (floats - center) * inverse
    normed = scaled.astype(jnp.bfloat16)
    mix_float = mixing.astype(jnp.float32)
    grad_mixed = lax.dot_general(upstream, w_output, (((1,), (1,)), ((), ())), preferred_element_type=jnp.float32).astype(jnp.bfloat16)
    grad_value = jnp.einsum('hij,ihd->jhd', mix_float, grad_mixed.reshape(length, heads_count, -1).astype(jnp.float32))
    grad_value = grad_value.astype(jnp.bfloat16).reshape(length, -1)
    grad_normed = lax.dot_general(grad_value, w_value, (((1,), (1,)), ((), ())), preferred_element_type=jnp.float32)
    first_mean = lax.optimization_barrier(jnp.mean(grad_normed, axis=-1, keepdims=True))
    second_mean = lax.optimization_barrier(jnp.mean(grad_normed * scaled, axis=-1, keepdims=True))
    grad_input = (upstream.astype(jnp.float32) + inverse * (grad_normed - first_mean - scaled * second_mean)).astype(jnp.bfloat16)
    value_term = lax.dot_general(normed, grad_value, (((0,), (0,)), ((), ())), preferred_element_type=jnp.float32)
    return (grad_input, value_term)

def reference(parked, arriving, slot_table, value_weight, output_weight, slopes):
    sections_count = parked.shape[0]
    slots_count = parked.shape[1]
    mixing = mixing_weights(slopes, parked.shape[2])
    sent_list = []
    value_list = []
    from_above = []
    for section_index in reversed(range(sections_count)):
        produced = []
        value_total = jnp.zeros(value_weight.shape[1:], jnp.float32)
        for window_slot in range(slots_count):
            if window_slot == 0:
                upstream = arriving[section_index]
            elif from_above:
                upstream = from_above[window_slot - 1]
            else:
                upstream = jnp.zeros_like(arriving[section_index])
            chosen = slot_table[section_index, window_slot].astype(jnp.int32)
            inputs = lax.dynamic_index_in_dim(parked[sections_count - 1 - section_index], chosen, 0, keepdims=False)
            grad_input, value_term = layer_step(inputs, upstream, value_weight[section_index], output_weight[section_index], mixing)
            produced.append(grad_input)
            value_total = value_total + value_term
        sent_list.append(produced[-1])
        value_list.append(value_total.astype(jnp.bfloat16))
        from_above = produced
    return (jnp.stack(sent_list[::-1]), jnp.stack(value_list[::-1]))
```

```python
import jax
import jax.numpy as jnp
from jax import lax
from jax.experimental import pallas as pl
from jax.experimental.pallas import tpu as pltpu
from jax.sharding import PartitionSpec as P

EPSILON = 1e-05
F32, BF16 = jnp.float32, jnp.bfloat16
NT = (((1,), (1,)), ((), ()))
TN = (((0,), (0,)), ((), ()))
NN = (((1,), (0,)), ((), ()))
SCOPED = 20 << 20
SMEM = pl.BlockSpec(memory_space=pltpu.SMEM)
VMEM = pl.BlockSpec(memory_space=pltpu.VMEM)


def call(body, out_shape, operands, flops=0, aliases=None):
    size = lambda a: a.size * a.dtype.itemsize
    single = not isinstance(out_shape, (list, tuple))
    outs = [out_shape] if single else list(out_shape)
    moved = sum(size(a) for a in operands) + sum(size(a) for a in outs)
    return pl.pallas_call(
        body,
        in_specs=[SMEM] + [VMEM] * (len(operands) - 1),
        out_specs=VMEM if single else [VMEM] * len(outs),
        out_shape=out_shape,
        input_output_aliases=aliases or {},
        compiler_params=pltpu.CompilerParams(vmem_limit_bytes=SCOPED),
        cost_estimate=pl.CostEstimate(flops=flops, bytes_accessed=moved, transcendentals=0),
    )(*operands)


def shape(dims, dtype):
    return jax.ShapeDtypeStruct(tuple(dims), dtype)


def grad_mixed_part(scalars, pieces, w_output, other, offset, size, received=None):
    rows = sum(p.shape[0] for p in pieces)
    half = w_output.shape[0] // 2
    count = len(pieces)

    def body(s, *refs):
        ups = jnp.concatenate([r[...] for r in refs[:count]], axis=0)
        w = refs[count]
        core = 1 - s[0] if other else s[0]
        start = pl.multiple_of(core * half + offset, 128)
        part = lax.dot_general(ups, w[pl.ds(start, size), :], NT, preferred_element_type=F32)
        if other:
            refs[count + 1][...] = part.astype(BF16)
        else:
            part = part + refs[count + 1][...].astype(F32)
            refs[count + 2][...] = part
            refs[count + 3][...] = part.astype(BF16)

    flops = 2 * rows * size * w_output.shape[1]
    if other:
        return call(body, shape((rows, size), BF16), [scalars, *pieces, w_output], flops)
    outs = [shape((rows, size), F32), shape((rows, size), BF16)]
    return call(body, outs, [scalars, *pieces, w_output, received], flops)


def unmix(scalars, kept, received, mixing, first_head):
    rows, size = kept.shape
    count = len(received)
    heads = mixing.shape[0] * size // (mixing.shape[0] * 128)

    def body(s, *refs):
        mix, out = refs[count + 1], refs[count + 2]
        for h in range(size // 128):
            cols = slice(h * 128, (h + 1) * 128)
            total = refs[0][:, cols]
            for r in refs[1 : count + 1]:
                total = total + r[:, cols].astype(F32)
            out[:, cols] = lax.dot_general(
                mix[first_head + h], total.astype(BF16), TN, preferred_element_type=F32
            ).astype(BF16)

    return call(
        body, shape((rows, size), BF16), [scalars, kept, *received, mixing], 2 * heads * rows * rows * 128
    )


def grad_normed_part(scalars, grads, w_value, other, offset, total=None):
    rows, size = grads.shape
    half = w_value.shape[1] // 2
    width = w_value.shape[0]

    def body(s, v, w, *refs):
        core = 1 - s[0] if other else s[0]
        start = pl.multiple_of(core * half + offset, 128)
        term = lax.dot_general(v[...], w[:, pl.ds(start, size)], NT, preferred_element_type=F32)
        if total is not None:
            term = term + refs[0][...]
        refs[-1][...] = term

    operands = [scalars, grads, w_value] + ([] if total is None else [total])
    return call(body, shape((rows, width), F32), operands, 2 * rows * size * width)


def grad_normed_last(scalars, grads, w_value, other, offset, total, inputs, pieces):
    rows, size = grads.shape
    half = w_value.shape[1] // 2
    width = w_value.shape[0]
    own = rows // pieces

    def body(s, v, w, total_ref, in_ref, keep, stats, *sends):
        core = 1 - s[0] if other else s[0]
        start = pl.multiple_of(core * half + offset, 128)
        term = lax.dot_general(v[...], w[:, pl.ds(start, size)], NT, preferred_element_type=F32)
        term = term + total_ref[...]
        keep[...] = term[:own]
        for t, ref in enumerate(sends):
            ref[...] = term[(t + 1) * own : (t + 2) * own].astype(BF16)
        stats[...] = stacked(
            [
                jnp.sum(term, axis=1, keepdims=True),
                jnp.sum(term * in_ref[...].astype(F32), axis=1, keepdims=True),
            ]
        )

    outs = [shape((own, width), F32), shape((8, rows), F32)]
    outs += [shape((own, width), BF16)] * (pieces - 1)
    operands = [scalars, grads, w_value, total, inputs]
    return call(body, outs, operands, 2 * rows * size * width)


def stacked(columns):
    rows = columns[0].shape[0]
    lane = lax.broadcasted_iota(jnp.int32, (rows, 128), 1)
    wide = jnp.zeros((rows, 128), F32)
    for k, column in enumerate(columns):
        wide = jnp.where(lane == k, column, wide)
    return wide.T[:8]


def as_columns(stats):
    rows = stats.shape[1]
    return jnp.concatenate([stats, jnp.zeros((120, rows), F32)], axis=0).T


def order_inputs(scalars, stores):
    slots, own, width = stores[0].shape
    count = len(stores)
    rows = own * count

    def body(s, *refs):
        outs, stats = refs[count : count + slots], refs[count + slots]
        columns = []
        for k in range(slots):
            picked = jnp.concatenate([r[s[1 + k]] for r in refs[:count]], axis=0)
            outs[k][...] = picked
            floats = picked.astype(F32)
            columns += [
                jnp.sum(floats, axis=1, keepdims=True),
                jnp.sum(floats * floats, axis=1, keepdims=True),
            ]
        stats[...] = stacked(columns)

    outs = [shape((rows, width), BF16)] * slots + [shape((8, rows), F32)]
    return call(body, outs, [scalars, *stores])


def normalize(scalars, inputs, stats, width):
    slots, (rows, part) = len(inputs), inputs[0].shape
    count = len(stats)

    def body(s, *refs):
        total = refs[slots][...]
        for r in refs[slots + 1 : slots + count]:
            total = total + r[...]
        columns = as_columns(total)
        for k in range(slots):
            center = columns[:, 2 * k : 2 * k + 1] / width
            inverse = lax.rsqrt(columns[:, 2 * k + 1 : 2 * k + 2] / width - center * center + EPSILON)
            floats = refs[k][...].astype(F32)
            refs[slots + count][k * rows : (k + 1) * rows, :] = ((floats - center) * inverse).astype(BF16)

    return call(body, shape((slots * rows, part), BF16), [scalars, *inputs, *stats])


def finish(scalars, keep, received, upstream, inputs, slot, input_stats, grad_stats, crossed, width):
    own, part = keep.shape
    rows = inputs.shape[0]
    n_in, n_grad, n_recv = len(input_stats), len(grad_stats), len(received)

    def body(s, keep_ref, ups_ref, in_ref, *refs):
        recv = refs[:n_recv]
        ins = refs[n_recv : n_recv + n_in]
        grads = refs[n_recv + n_in : n_recv + n_in + n_grad]
        out = refs[-1]
        total_in = ins[0][...]
        for r in ins[1:]:
            total_in = total_in + r[...]
        total = grads[0][...]
        for r, t in zip(grads[1:], crossed[1:], strict=True):
            got = r[...]
            if t:
                got = jnp.concatenate(
                    [got[:, (b ^ t) * own : ((b ^ t) + 1) * own] for b in range(rows // own)], axis=1
                )
            total = total + got
        in_columns = as_columns(total_in)[:own]
        columns = as_columns(total)[:own]
        center = in_columns[:, 2 * slot : 2 * slot + 1] / width
        inverse = lax.rsqrt(in_columns[:, 2 * slot + 1 : 2 * slot + 2] / width - center * center + EPSILON)
        first = columns[:, 0:1]
        second = (columns[:, 1:2] - center * first) * inverse
        grad = keep_ref[...]
        for r in recv:
            grad = grad + r[...].astype(F32)
        scaled = (in_ref[:own].astype(F32) - center) * inverse
        out[...] = (
            ups_ref[...].astype(F32) + inverse * (grad - first / width - scaled * (second / width))
        ).astype(BF16)

    operands = [scalars, keep, upstream, inputs, *received, *input_stats, *grad_stats]
    return call(body, shape((own, part), BF16), operands)


def value_grad_part(scalars, normed, grads, result, dims, other, offset):
    depth, width = normed.shape
    size = grads[0].shape[1]
    half = dims[1] // 2
    block = width // 3 if width % 3 == 0 and width // 3 % 128 == 0 else width // 2
    count = len(grads)

    def body(s, n, *refs):
        v = jnp.concatenate([r[...] for r in refs[:count]], axis=0)
        refs[-1][...] = lax.dot_general(n[...], v, TN, preferred_element_type=F32).astype(BF16)

    def place(i, s):
        core = 1 - s[0] if other else s[0]
        return (i, core * (half // size) + offset // size)

    in_specs = [pl.BlockSpec((depth, block), lambda i, s: (0, i))]
    in_specs += [pl.BlockSpec(g.shape, lambda i, s: (0, 0)) for g in grads]
    operands = [scalars, normed, *grads]
    aliases = {}
    if result is not None:
        in_specs.append(pl.BlockSpec(memory_space=pl.ANY))
        aliases = {len(operands): 0}
        operands.append(result)
    return pl.pallas_call(
        body,
        grid_spec=pltpu.PrefetchScalarGridSpec(
            num_scalar_prefetch=1,
            grid=(width // block,),
            in_specs=in_specs,
            out_specs=pl.BlockSpec((block, size), place),
        ),
        out_shape=shape(dims, BF16),
        input_output_aliases=aliases,
        compiler_params=pltpu.CompilerParams(vmem_limit_bytes=SCOPED),
        cost_estimate=pl.CostEstimate(
            flops=2 * depth * width * size, bytes_accessed=2 * width * size, transcendentals=0
        ),
    )(*operands)


def mixing_weights(slopes, places):
    distance = (places[:, None] - places[None, :]).astype(F32)
    causal = distance >= 0
    logits = -slopes[:, None, None] * jnp.where(causal, distance, 0.0)[None, :, :]
    weights = jnp.where(causal[None, :, :], jnp.exp(logits), 0.0)
    return (weights / jnp.sum(weights, axis=-1, keepdims=True)).astype(BF16)


def flipped(array, axis, mask):
    return lax.ppermute(array, axis, [(i, i ^ mask) for i in range(lax.axis_size(axis))])


def on_device(parked, arriving, slot_table, value_weight, output_weight, slopes):
    sections, tensors, parts = (lax.axis_size(a) for a in ("section", "tensor", "dp"))
    section, tensor, part = (lax.axis_index(a) for a in ("section", "tensor", "dp"))
    core = part % 2
    w_value = pltpu.with_memory_space_constraint(value_weight[0], pltpu.VMEM)
    w_output = pltpu.with_memory_space_constraint(output_weight[0], pltpu.VMEM)
    slots, own, part_width = parked.shape[1:]
    width = part_width * parts
    half = w_output.shape[0] // 2
    others = range(1, tensors)
    chips = range(2, parts, 2)
    bounds = [0, half // 2, half]
    chunks = [(a, b - a) for a, b in zip(bounds[:-1], bounds[1:], strict=True)]

    table = lax.dynamic_index_in_dim(slot_table, section, 0, keepdims=False)
    scalars = jnp.concatenate([core[None], table]).astype(jnp.int32)

    upstream = arriving[0]
    pieces = [upstream] + [flipped(upstream, "tensor", t) for t in others]
    store = lax.ppermute(parked[0], "section", [(i, sections - 1 - i) for i in range(sections)])
    stores = [store] + [flipped(store, "tensor", t) for t in others]

    blocks = jnp.arange(tensors) ^ tensor
    places = (blocks[:, None] * own + jnp.arange(own)[None, :]).reshape(-1)
    heads = slopes.shape[0] // 2
    mixing = mixing_weights(lax.dynamic_slice_in_dim(slopes, core * heads, heads), places)

    ordered = order_inputs(scalars, stores)
    inputs, stats = ordered[:slots], ordered[slots]
    stats = stats + flipped(stats, "dp", 1)
    input_stats = [stats] + [flipped(stats, "dp", m) for m in chips]

    values = []
    for slot in range(slots):
        if slot > 0:
            pieces = [
                lax.ppermute(
                    upstream,
                    ("section", "tensor"),
                    [(i * tensors + j, (i - 1) * tensors + (j ^ t)) for i in range(1, sections) for j in range(tensors)],
                )
                for t in range(tensors)
            ]
            upstream = pieces[0]
        sends = [grad_mixed_part(scalars, pieces, w_output, True, a, n) for a, n in chunks]
        halves = [flipped(x, "dp", 1) for x in sends]
        kept = [
            grad_mixed_part(scalars, pieces, w_output, False, a, n, x)
            for (a, n), x in zip(chunks, halves, strict=True)
        ]
        across = [[flipped(x, "dp", m) for m in chips] for _, x in kept]
        mine = [
            unmix(scalars, k, x, mixing, a // 128)
            for (k, _), x, (a, n) in zip(kept, across, chunks, strict=True)
        ]
        theirs = [flipped(x, "dp", 1) for x in mine]
        values.append([mine, theirs])
        total = None
        for j, (a, n) in enumerate(chunks):
            total = grad_normed_part(scalars, mine[j], w_value, False, a, total)
            if j + 1 < len(chunks):
                total = grad_normed_part(scalars, theirs[j], w_value, True, a, total)
        keep, stats, *sends = grad_normed_last(
            scalars, theirs[-1], w_value, True, chunks[-1][0], total, inputs[slot], tensors
        )
        received = [flipped(x, "tensor", t) for t, x in zip(others, sends, strict=True)]
        stats = stats + flipped(stats, "dp", 1)
        routes = [(t, m) for t in range(tensors) for m in range(0, parts, 2) if t or m]
        grad_stats = [stats] + [flipped(stats, ("tensor", "dp"), t * parts + m) for t, m in routes]
        upstream = finish(
            scalars, keep, received, upstream, inputs[slot], slot, input_stats, grad_stats,
            [0] + [t for t, _ in routes], width,
        )

    normed = normalize(scalars, inputs, input_stats, width)
    result = None
    for j, (a, n) in enumerate(chunks):
        for side in range(2):
            result = value_grad_part(
                scalars, normed, [v[side][j] for v in values], result, w_value.shape, side == 1, a
            )
    return (upstream[None], result[None])


def solution(mesh):
    in_specs = (
        P("section", None, "tensor", "dp"),
        P("section", "tensor", "dp"),
        P(),
        P("section", "dp", "tensor"),
        P("section", "tensor", "dp"),
        P("tensor"),
    )
    out_specs = (P("section", "tensor", "dp"), P("section", "dp", "tensor"))
    return jax.shard_map(
        on_device, mesh=mesh, in_specs=in_specs, out_specs=out_specs, check_vma=False
    )
```

```python
import jax
import jax.numpy as jnp
from jax import lax
from jax.experimental import pallas as pl
from jax.experimental.pallas import tpu as pltpu
from jax.sharding import PartitionSpec as P

EPSILON = 1e-05
F32, BF16 = jnp.float32, jnp.bfloat16
NT = (((1,), (1,)), ((), ()))
TN = (((0,), (0,)), ((), ()))
SCOPED = 14 << 20
SMEM = pl.BlockSpec(memory_space=pltpu.SMEM)
VMEM = pl.BlockSpec(memory_space=pltpu.VMEM)
ANY = pl.BlockSpec(memory_space=pl.ANY)
HEAD = 128
STEPS = 8
COST = pl.CostEstimate(flops=10**10, bytes_accessed=10**8, transcendentals=0)


def call(body, outs, operands, held=(), first_spec=VMEM, carry=()):
    operands = list(operands)
    held = [h for h in held if not any(h is a for a in operands)]
    n_in, n_held, n_out, n_carry = len(operands), len(held), len(outs), len(carry)
    sources = [pltpu.with_memory_space_constraint(w, pltpu.HBM) for w, _, _, _ in carry]
    rows = carry[0][0].shape[0] if carry else 0
    block = rows // STEPS

    def kernel(*refs):
        ins, refs = refs[:n_in], refs[n_in + n_held :]
        weights, refs = refs[:n_carry], refs[n_carry:]
        made, refs = refs[:n_out], refs[n_out:]
        copies = []
        for k, (w, (_, other, offset, size)) in enumerate(zip(weights, carry, strict=True)):
            columns = w.shape[1]
            start = 0 if size == columns else half_start(columns, other, offset)
            for i in range(STEPS):
                part = pl.ds(i * block, block)
                source = w.at[part] if size == columns else w.at[part, pl.ds(start, size)]
                copies.append(pltpu.make_async_copy(source, refs[k].at[part], refs[n_carry].at[k, i]))
        for copy in copies:
            copy.start()
        if body is not None:
            body(*ins, *made)
        for copy in copies:
            copy.wait()

    more = [pltpu.VMEM((rows, size), w.dtype) for w, _, _, size in carry]
    return pl.pallas_call(
        kernel,
        in_specs=([first_spec] + [VMEM] * (n_in - 1) if n_in else [])
        + [VMEM] * n_held
        + [pl.BlockSpec(memory_space=pltpu.HBM)] * n_carry,
        out_specs=[VMEM] * (n_out + n_carry),
        out_shape=[*outs, *more],
        scratch_shapes=[pltpu.SemaphoreType.DMA((n_carry, STEPS))] if carry else [],
        compiler_params=pltpu.CompilerParams(vmem_limit_bytes=SCOPED),
        cost_estimate=COST,
    )(*operands, *held, *sources)


def shape(dims, dtype):
    return jax.ShapeDtypeStruct(tuple(dims), dtype)


def after(array, *earlier):
    return lax.optimization_barrier((array, *earlier))[0]


def half_start(extent, other, offset):
    core = lax.axis_index("dp") % 2
    core = 1 - core if other else core
    return pl.multiple_of(core * (extent // 2) + offset, HEAD)


def grad_mixed_part(pieces, w_output, other, offset, size, received=None, held=(), carry=()):
    counts = [len(p) for p in pieces]
    flat = [a for p in pieces for a in p]
    rows = sum(p[0].shape[0] for p in pieces)

    def body(*refs):
        blocks, at = [], 0
        for n in counts:
            blocks.append(jnp.concatenate([r[...] for r in refs[at : at + n]], axis=1))
            at += n
        ups = jnp.concatenate(blocks, axis=0)
        w = refs[at]
        start = half_start(w_output.shape[0], other, offset)
        part = lax.dot_general(ups, w[pl.ds(start, size), :], NT, preferred_element_type=F32)
        if other:
            refs[at + 1][...] = part.astype(BF16)
        else:
            part = part + refs[at + 1][...].astype(F32)
            refs[at + 2][...] = part
            refs[at + 3][...] = part.astype(BF16)

    if other:
        return call(body, [shape((rows, size), BF16)], [*flat, w_output], held, carry=carry)
    outs = [shape((rows, size), F32), shape((rows, size), BF16)]
    return call(body, outs, [*flat, w_output, received], held, carry=carry)


def unmix(kept, received, mixing, first_head, held=()):
    rows, size = kept.shape
    count = len(received)

    def body(*refs):
        mix, out = refs[count + 1], refs[count + 2]
        for h in range(size // HEAD):
            cols = slice(h * HEAD, (h + 1) * HEAD)
            total = refs[0][:, cols]
            for r in refs[1 : count + 1]:
                total = total + r[:, cols].astype(F32)
            out[:, cols] = lax.dot_general(
                mix[first_head + h], total.astype(BF16), TN, preferred_element_type=F32
            ).astype(BF16)

    return call(body, [shape((rows, size), BF16)], [kept, *received, mixing], held)


def grad_normed_part(grads, weights, total=None, pieces=0, held=(), carry=()):
    rows, width = grads[0].shape[0], weights[0].shape[0]
    count = len(grads)

    def body(*refs):
        sums = None if total is None else refs[2 * count][...]
        for g, w in zip(refs[:count], refs[count : 2 * count], strict=True):
            term = lax.dot_general(g[...], w[...], NT, preferred_element_type=F32)
            sums = term if sums is None else sums + term
        if not pieces:
            refs[-1][...] = sums
            return
        keep, *sends = refs[-pieces:]
        own = rows // pieces
        keep[...] = sums[:own]
        for t, ref in enumerate(sends):
            ref[...] = sums[(t + 1) * own : (t + 2) * own].astype(BF16)

    if pieces:
        outs = [shape((rows // pieces, width), F32)] + [shape((rows // pieces, width), BF16)] * (pieces - 1)
    else:
        outs = [shape((rows, width), F32)]
    operands = [*grads, *weights] + ([] if total is None else [total])
    return call(body, outs, operands, held, carry=carry)


def stacked(columns):
    rows = columns[0].shape[0]
    lane = lax.broadcasted_iota(jnp.int32, (rows, 128), 1)
    wide = jnp.zeros((rows, 128), F32)
    for k, column in enumerate(columns):
        wide = jnp.where(lane == k, column, wide)
    if rows % 128:
        wide = jnp.concatenate([wide, jnp.zeros((-rows % 128, 128), F32)], axis=0)
    return wide.T[:8]


def as_columns(stats, rows):
    return jnp.concatenate([stats, jnp.zeros((120, stats.shape[1]), F32)], axis=0).T[:rows]


def added(one, other, held=()):
    def body(a, b, out):
        out[...] = a[...] + b[...]

    return call(body, [shape(one.shape, one.dtype)], [one, other], held)


def ordered(store, table, held=()):
    slots = store.shape[0]

    def body(s, store_ref, *outs):
        for k, out in enumerate(outs):
            out[...] = store_ref[s[k]]

    return call(body, [shape(store.shape[1:], BF16)] * slots, [table, store], held, SMEM)


def width_sums(keep, received, inputs, slot, held=()):
    own, width = keep.shape
    slots = len(inputs)

    def body(keep_ref, *refs):
        ins, refs = refs[:slots], refs[slots:]
        grad_ref, stats = refs[-2:]
        grad = keep_ref[...]
        for r in refs[:-2]:
            grad = grad + r[...].astype(F32)
        grad_ref[...] = grad
        floats = [r[...].astype(F32) for r in ins]
        columns = [jnp.sum(grad, axis=1, keepdims=True), jnp.sum(grad * floats[slot], axis=1, keepdims=True)]
        if slot == 0:
            for x in floats:
                columns += [jnp.sum(x, axis=1, keepdims=True), jnp.sum(x * x, axis=1, keepdims=True)]
        stats[...] = stacked(columns)

    outs = [shape((own, width), F32), shape((8, -(-own // 128) * 128), F32)]
    return call(body, outs, [keep, *inputs, *received], held)


def finish(grad, upstream, inputs, slot, input_stats, grad_stats, width, parts, held=()):
    own, part = grad.shape
    slots = len(inputs)
    n_up, n_in, n_grad = len(upstream), len(input_stats), len(grad_stats)

    def body(grad_ref, *refs):
        x_refs, refs = refs[:slots], refs[slots:]
        ups, refs = refs[:n_up], refs[n_up:]
        ins, refs = refs[:n_in], refs[n_in:]
        grads, outs = refs[:n_grad], refs[n_grad:]
        total_in = ins[0][...]
        for r in ins[1:]:
            total_in = total_in + r[...]
        total = grads[0][...]
        for r in grads[1:]:
            total = total + r[...]
        in_columns = as_columns(total_in, own)
        columns = as_columns(total, own)

        def normal(k):
            center = in_columns[:, 2 * k + 2 : 2 * k + 3] / width
            inverse = lax.rsqrt(in_columns[:, 2 * k + 3 : 2 * k + 4] / width - center * center + EPSILON)
            return center, inverse, (x_refs[k][...].astype(F32) - center) * inverse

        center, inverse, scaled = normal(slot)
        first = columns[:, 0:1]
        second = (columns[:, 1:2] - center * first) * inverse
        above = jnp.concatenate([r[...] for r in ups], axis=1).astype(F32)
        made = (above + inverse * (grad_ref[...] - first / width - scaled * (second / width))).astype(BF16)
        for k in range(parts):
            outs[k][...] = made[:, k * (part // parts) : (k + 1) * (part // parts)]
        if slot == 0:
            for k in range(slots):
                outs[parts + k][...] = (scaled if k == slot else normal(k)[2]).astype(BF16)

    operands = [grad, *inputs, *upstream, *input_stats, *grad_stats]
    outs = [shape((own, part // parts), BF16)] * parts
    if slot == 0:
        outs += [shape((own, part), BF16)] * slots
    return call(body, outs, operands, held)


def value_grad_part(normed, grads, result, dims, other, offset):
    depth, width = sum(a.shape[0] for a in normed), normed[0].shape[1]
    blocks = len(normed)
    size = grads[0].shape[1]
    count = len(grads)
    block = 256 if width % 256 == 0 else 128
    steps = width // block
    given = [] if result is None else [result]

    def body(*refs):
        norms, refs = refs[:blocks], refs[blocks:]
        out, made, sems = refs[count + len(given) :]
        v = jnp.concatenate([r[...] for r in refs[:count]], axis=0)
        start = half_start(dims[1], other, offset)
        copies = []
        for i in range(steps):
            rows = pl.ds(i * block, block)
            made[rows, :] = lax.dot_general(
                jnp.concatenate([n[:, i * block : (i + 1) * block] for n in norms], axis=0),
                v,
                TN,
                preferred_element_type=F32,
            ).astype(BF16)
            copies.append(
                pltpu.make_async_copy(made.at[rows], out.at[rows, pl.ds(start, size)], sems.at[i])
            )
            copies[-1].start()
        for copy in copies:
            copy.wait()

    return pl.pallas_call(
        body,
        in_specs=[VMEM] * (blocks + count) + [ANY] * len(given),
        out_specs=ANY,
        out_shape=pltpu.HBM(dims, BF16),
        scratch_shapes=[pltpu.VMEM((width, size), BF16), pltpu.SemaphoreType.DMA((steps,))],
        input_output_aliases={blocks + count: 0} if given else {},
        compiler_params=pltpu.CompilerParams(vmem_limit_bytes=SCOPED),
        cost_estimate=COST,
    )(*normed, *grads, *given)


def mixing_weights(slopes, length, own, held=()):
    heads = slopes.shape[0] // 2

    def body(slopes_ref, out):
        tensor = lax.axis_index("tensor")
        first = (lax.axis_index("dp") % 2) * heads

        def place(dim):
            local = lax.broadcasted_iota(jnp.int32, (length, length), dim)
            return ((local // own) ^ tensor) * own + local % own

        distance = (place(0) - place(1)).astype(F32)
        causal = distance >= 0
        distance = jnp.where(causal, distance, 0.0)
        for h in range(heads):
            logits = -slopes_ref[pl.ds(first + h, 1), :] * distance
            weights = jnp.where(causal, jnp.exp(logits), 0.0)
            out[h] = (weights / jnp.sum(weights, axis=-1, keepdims=True)).astype(BF16)

    wide = jnp.broadcast_to(slopes[:, None], (slopes.shape[0], length))
    return call(body, [shape((heads, length, length), BF16)], [wide], held)


def flipped(array, axis, mask):
    return lax.ppermute(array, axis, [(i, i ^ mask) for i in range(lax.axis_size(axis))])


def on_device(parked, arriving, slot_table, value_weight, output_weight, slopes):
    sections, tensors, parts = (lax.axis_size(a) for a in ("section", "tensor", "dp"))
    slots, own, part_width = parked.shape[1:]
    width = part_width * parts
    half = output_weight.shape[1] // 2
    others = range(1, tensors)
    chips = range(2, parts, 2)
    bounds = [0, half // 2, half]
    chunks = [(a, b - a) for a, b in zip(bounds[:-1], bounds[1:], strict=True)]
    final = len(chunks) - 1

    def others_of(array):
        return [flipped(array, "tensor", t) for t in others]

    token, held = [None], []

    def run(kernel, first, *rest, **more):
        if token[0] is not None:
            if isinstance(first, list):
                first = [after(first[0], token[0]), *first[1:]]
            else:
                first = after(first, token[0])
        outs = kernel(first, *rest, held=held, **more)
        token[0] = outs[0]
        return outs

    upstream = [arriving[0]]
    pieces = [[a] for a in [upstream[0], *others_of(upstream[0])]]
    table = lax.dynamic_index_in_dim(slot_table, lax.axis_index("section"), 0, keepdims=False)
    mixing, = run(mixing_weights, after(slopes, table), own * tensors, own)
    w_output, = run(
        lambda w, held: call(None, [], [], held, carry=[(w, False, 0, w.shape[1])]), output_weight[0]
    )
    held.append(w_output)
    w_value = [[None, None] for _ in chunks]

    def spans(j, sides):
        return [(value_weight[0], side == 1, *chunks[j]) for side in sides]

    values, input_stats, result = [], None, None
    for slot in range(slots):
        last = slot == slots - 1
        if slot > 0:
            upstream = [lax.ppermute(a, "section", [(i, i - 1) for i in range(1, sections)]) for a in upstream]
            pieces = [list(p) for p in zip(*[[a, *others_of(a)] for a in upstream], strict=True)]

        def product(j, other, received=None, carry=()):
            a, n = chunks[j]
            mixed = lambda first, *rest, held: grad_mixed_part([first, *pieces[1:]], *rest, held, carry)
            return run(mixed, pieces[0], w_output, other, a, n, received)

        halves, kept, across = [], [], []
        for j in range(len(chunks) + 1):
            if j <= final:
                halves.append(flipped(product(j, True)[0], "dp", 1))
            if j > 0:
                bring = slot == 0 and j - 1 == final
                outs = product(j - 1, False, halves[j - 1], spans(0, (0, 1)) if bring else ())
                if bring:
                    w_value[0] = outs[2:]
                    held.extend(outs[2:])
                kept.append(outs[:2])
                across.append([flipped(outs[1], "dp", m) for m in chips])
        if slot == 0:
            store = lax.ppermute(
                after(parked[0], kept[-1][1]), "section", [(i, sections - 1 - i) for i in range(sections)]
            )
        mine, theirs, total = [], [], None
        for j, (a, n) in enumerate(chunks):
            mine += run(unmix, kept[j][0], across[j], mixing, a // HEAD)
            theirs.append(flipped(mine[j], "dp", 1))
            for side, grads in enumerate((mine[j], theirs[j])):
                end = j == final and side == 1
                bring = slot == 0 and j < final
                outs = run(
                    grad_normed_part, [grads], [w_value[j][side]], total, tensors if end else 0,
                    carry=spans(j + 1, (side,)) if bring else (),
                )
                if bring:
                    w_value[j + 1][side] = outs[-1]
                    held.append(outs[-1])
                if end:
                    keep, *sends = outs
                else:
                    total = outs[0]
        values.append([mine, theirs])
        received = [flipped(x, "tensor", t) for t, x in zip(others, sends, strict=True)]
        if last:
            held.clear()
        if slot == 0:
            inputs = run(ordered, store, table)
        grad, sums = run(width_sums, keep, received, inputs, slot)
        sums, = run(added, sums, flipped(sums, "dp", 1))
        grad_stats = [sums] + [flipped(sums, "dp", m) for m in chips]
        if slot == 0:
            input_stats = grad_stats
        outs = run(finish, grad, upstream, inputs, slot, input_stats, grad_stats, width, 1 if last else 2)
        if slot == 0:
            normed = outs[-slots:]
            outs = outs[:-slots]
        upstream = outs

    normed = [b for a in normed for b in [a, *others_of(a)]]
    result = None
    for j, (a, n) in enumerate(chunks):
        for side in range(2):
            result = value_grad_part(
                normed, [v[side][j] for v in values], result, value_weight.shape[1:], side == 1, a
            )
    return (upstream[0][None], result[None])


def solution(mesh):
    in_specs = (
        P("section", None, "tensor", "dp"),
        P("section", "tensor", "dp"),
        P(),
        P("section", "dp", "tensor"),
        P("section", "tensor", "dp"),
        P("tensor"),
    )
    out_specs = (P("section", "tensor", "dp"), P("section", "dp", "tensor"))
    return jax.shard_map(
        on_device, mesh=mesh, in_specs=in_specs, out_specs=out_specs, check_vma=False
    )
```

```python
import jax
import jax.numpy as jnp
from jax import lax
from jax.experimental import pallas as pl
from jax.experimental.pallas import tpu as pltpu
from jax.sharding import PartitionSpec as P

EPSILON = 1e-05
F32, BF16 = jnp.float32, jnp.bfloat16
NT = (((1,), (1,)), ((), ()))
TN = (((0,), (0,)), ((), ()))
SCOPED = 14 << 20
SMEM = pl.BlockSpec(memory_space=pltpu.SMEM)
VMEM = pl.BlockSpec(memory_space=pltpu.VMEM)
ANY = pl.BlockSpec(memory_space=pl.ANY)
HEAD = 128
STEPS = 8
COST = pl.CostEstimate(flops=4 * 10**9, bytes_accessed=10**8, transcendentals=0)
LIGHT = pl.CostEstimate(flops=1, bytes_accessed=1, transcendentals=0)


def call(body, outs, operands, held=(), first_spec=VMEM, carry=(), light=False):
    operands = list(operands)
    held = [h for h in held if not any(h is a for a in operands)]
    n_in, n_held, n_out, n_carry = len(operands), len(held), len(outs), len(carry)
    sources = [pltpu.with_memory_space_constraint(w, pltpu.HBM) for w, _, _, _ in carry]
    rows = carry[0][0].shape[0] if carry else 0
    block = rows // STEPS

    def kernel(*refs):
        ins, refs = refs[:n_in], refs[n_in + n_held :]
        weights, refs = refs[:n_carry], refs[n_carry:]
        made, refs = refs[:n_out], refs[n_out:]
        copies = []
        for k, (w, (_, other, offset, size)) in enumerate(zip(weights, carry, strict=True)):
            columns = w.shape[1]
            start = 0 if size == columns else half_start(columns, other, offset)
            for i in range(STEPS):
                part = pl.ds(i * block, block)
                source = w.at[part] if size == columns else w.at[part, pl.ds(start, size)]
                copies.append(pltpu.make_async_copy(source, refs[k].at[part], refs[n_carry].at[k, i]))
        for copy in copies:
            copy.start()
        if body is not None:
            body(*ins, *made)
        for copy in copies:
            copy.wait()

    more = [pltpu.VMEM((rows, size), w.dtype) for w, _, _, size in carry]
    return pl.pallas_call(
        kernel,
        in_specs=([first_spec] + [VMEM] * (n_in - 1) if n_in else [])
        + [VMEM] * n_held
        + [pl.BlockSpec(memory_space=pltpu.HBM)] * n_carry,
        out_specs=[VMEM] * (n_out + n_carry),
        out_shape=[*outs, *more],
        scratch_shapes=[pltpu.SemaphoreType.DMA((n_carry, STEPS))] if carry else [],
        compiler_params=pltpu.CompilerParams(vmem_limit_bytes=SCOPED),
        cost_estimate=LIGHT if light else COST,
    )(*operands, *held, *sources)


def shape(dims, dtype):
    return jax.ShapeDtypeStruct(tuple(dims), dtype)


def after(array, *earlier):
    return lax.optimization_barrier((array, *earlier))[0]


def half_start(extent, other, offset):
    core = lax.axis_index("dp") % 2
    core = 1 - core if other else core
    return pl.multiple_of(core * (extent // 2) + offset, HEAD)


def grad_mixed_part(pieces, w_output, other, offset, size, received=None, held=(), carry=()):
    counts = [len(p) for p in pieces]
    flat = [a for p in pieces for a in p]
    rows = sum(p[0].shape[0] for p in pieces)

    def body(*refs):
        blocks, at = [], 0
        for n in counts:
            blocks.append(jnp.concatenate([r[...] for r in refs[at : at + n]], axis=1))
            at += n
        ups = jnp.concatenate(blocks, axis=0)
        w = refs[at]
        start = half_start(w_output.shape[0], other, offset)
        part = lax.dot_general(ups, w[pl.ds(start, size), :], NT, preferred_element_type=F32)
        if other:
            refs[at + 1][...] = part.astype(BF16)
        else:
            part = part + refs[at + 1][...].astype(F32)
            refs[at + 2][...] = part
            refs[at + 3][...] = part.astype(BF16)

    if other:
        return call(body, [shape((rows, size), BF16)], [*flat, w_output], held, carry=carry)
    outs = [shape((rows, size), F32), shape((rows, size), BF16)]
    return call(body, outs, [*flat, w_output, received], held, carry=carry)


def unmix(kept, received, mixing, first_head, held=()):
    rows, size = kept.shape
    count = len(received)

    def body(*refs):
        mix, out = refs[count + 1], refs[count + 2]
        for h in range(size // HEAD):
            cols = slice(h * HEAD, (h + 1) * HEAD)
            total = refs[0][:, cols]
            for r in refs[1 : count + 1]:
                total = total + r[:, cols].astype(F32)
            out[:, cols] = lax.dot_general(
                mix[first_head + h], total.astype(BF16), TN, preferred_element_type=F32
            ).astype(BF16)

    return call(body, [shape((rows, size), BF16)], [kept, *received, mixing], held)


def grad_normed_part(grads, w_value, other, offset, total=None, pieces=0, held=()):
    (rows, size), width = grads.shape, w_value.shape[0]

    def body(v, w, *refs):
        start = half_start(w_value.shape[1], other, offset)
        sums = lax.dot_general(v[...], w[:, pl.ds(start, size)], NT, preferred_element_type=F32)
        if total is not None:
            sums = sums + refs[0][...]
        if not pieces:
            refs[-1][...] = sums
            return
        keep, *sends = refs[-pieces:]
        own = rows // pieces
        keep[...] = sums[:own]
        for t, ref in enumerate(sends):
            ref[...] = sums[(t + 1) * own : (t + 2) * own].astype(BF16)

    if pieces:
        outs = [shape((rows // pieces, width), F32)] + [shape((rows // pieces, width), BF16)] * (pieces - 1)
    else:
        outs = [shape((rows, width), F32)]
    operands = [grads, pltpu.with_memory_space_constraint(w_value, pltpu.VMEM)] + ([] if total is None else [total])
    return call(body, outs, operands, held)


def stacked(columns):
    rows = columns[0].shape[0]
    lane = lax.broadcasted_iota(jnp.int32, (rows, 128), 1)
    wide = jnp.zeros((rows, 128), F32)
    for k, column in enumerate(columns):
        wide = jnp.where(lane == k, column, wide)
    if rows % 128:
        wide = jnp.concatenate([wide, jnp.zeros((-rows % 128, 128), F32)], axis=0)
    return wide.T[:8]


def as_columns(stats, rows):
    return jnp.concatenate([stats, jnp.zeros((120, stats.shape[1]), F32)], axis=0).T[:rows]


def added(one, other, held=()):
    def body(a, b, out):
        out[...] = a[...] + b[...]

    return call(body, [shape(one.shape, one.dtype)], [one, other], held)


def ordered(store, table, held=()):
    slots = store.shape[0]

    def body(s, store_ref, *outs):
        section = lax.axis_index("section")
        for k, out in enumerate(outs):
            out[...] = store_ref[s[k, section]]

    return call(body, [shape(store.shape[1:], BF16)] * slots, [table, store], held, SMEM, light=True)


def width_sums(keep, received, inputs, slot, held=()):
    own, width = keep.shape
    slots = len(inputs)

    def body(keep_ref, *refs):
        ins, refs = refs[:slots], refs[slots:]
        grad_ref, stats = refs[-2:]
        grad = keep_ref[...]
        for r in refs[:-2]:
            grad = grad + r[...].astype(F32)
        grad_ref[...] = grad
        floats = [r[...].astype(F32) for r in ins]
        columns = [jnp.sum(grad, axis=1, keepdims=True), jnp.sum(grad * floats[slot], axis=1, keepdims=True)]
        if slot == 0:
            for x in floats:
                columns += [jnp.sum(x, axis=1, keepdims=True), jnp.sum(x * x, axis=1, keepdims=True)]
        stats[...] = stacked(columns)

    outs = [shape((own, width), F32), shape((8, -(-own // 128) * 128), F32)]
    return call(body, outs, [keep, *inputs, *received], held)


def finish(grad, upstream, inputs, slot, input_stats, grad_stats, width, parts, held=()):
    own, part = grad.shape
    slots = len(inputs)
    n_up, n_in, n_grad = len(upstream), len(input_stats), len(grad_stats)

    def body(grad_ref, *refs):
        x_refs, refs = refs[:slots], refs[slots:]
        ups, refs = refs[:n_up], refs[n_up:]
        ins, refs = refs[:n_in], refs[n_in:]
        grads, outs = refs[:n_grad], refs[n_grad:]
        total_in = ins[0][...]
        for r in ins[1:]:
            total_in = total_in + r[...]
        total = grads[0][...]
        for r in grads[1:]:
            total = total + r[...]
        in_columns = as_columns(total_in, own)
        columns = as_columns(total, own)

        def normal(k):
            center = in_columns[:, 2 * k + 2 : 2 * k + 3] / width
            inverse = lax.rsqrt(in_columns[:, 2 * k + 3 : 2 * k + 4] / width - center * center + EPSILON)
            return center, inverse, (x_refs[k][...].astype(F32) - center) * inverse

        center, inverse, scaled = normal(slot)
        first = columns[:, 0:1]
        second = (columns[:, 1:2] - center * first) * inverse
        above = jnp.concatenate([r[...] for r in ups], axis=1).astype(F32)
        made = (above + inverse * (grad_ref[...] - first / width - scaled * (second / width))).astype(BF16)
        for k in range(parts):
            outs[k][...] = made[:, k * (part // parts) : (k + 1) * (part // parts)]
        if slot == 0:
            for k in range(slots):
                outs[parts + k][...] = (scaled if k == slot else normal(k)[2]).astype(BF16)

    operands = [grad, *inputs, *upstream, *input_stats, *grad_stats]
    outs = [shape((own, part // parts), BF16)] * parts
    if slot == 0:
        outs += [shape((own, part), BF16)] * slots
    return call(body, outs, operands, held)


def value_grad_part(normed, grads, result, dims, other, offset, held=()):
    depth, width = sum(a.shape[0] for a in normed), normed[0].shape[1]
    blocks = len(normed)
    size = grads[0].shape[1]
    count = len(grads)
    block = 256 if width % 256 == 0 else 128
    steps = width // block
    given = [] if result is None else [result]

    def body(*refs):
        norms, refs = refs[:blocks], refs[blocks:]
        out, made, sems = refs[count + len(given) :]
        v = jnp.concatenate([r[...] for r in refs[:count]], axis=0)
        start = half_start(dims[1], other, offset)
        copies = []
        for i in range(steps):
            rows = pl.ds(i * block, block)
            made[rows, :] = lax.dot_general(
                jnp.concatenate([n[:, i * block : (i + 1) * block] for n in norms], axis=0),
                v,
                TN,
                preferred_element_type=F32,
            ).astype(BF16)
            copies.append(
                pltpu.make_async_copy(made.at[rows], out.at[rows, pl.ds(start, size)], sems.at[i])
            )
            copies[-1].start()
        for copy in copies:
            copy.wait()

    return pl.pallas_call(
        body,
        in_specs=[VMEM] * (blocks + count) + [ANY] * len(given),
        out_specs=[ANY],
        out_shape=[pltpu.HBM(dims, BF16)],
        scratch_shapes=[pltpu.VMEM((width, size), BF16), pltpu.SemaphoreType.DMA((steps,))],
        input_output_aliases={blocks + count: 0} if given else {},
        compiler_params=pltpu.CompilerParams(vmem_limit_bytes=SCOPED),
        cost_estimate=COST,
    )(*normed, *grads, *given)


def mixing_and_weight(slopes, weight, length, own, held=()):
    heads = slopes.shape[1] // 2

    def body(slopes_ref, out):
        tensor = lax.axis_index("tensor")
        first = (lax.axis_index("dp") % 2) * heads

        def place(dim):
            local = lax.broadcasted_iota(jnp.int32, (length, length), dim)
            return ((local // own) ^ tensor) * own + local % own

        distance = (place(0) - place(1)).astype(F32)
        causal = distance >= 0
        distance = jnp.where(causal, distance, 0.0)
        lane = lax.broadcasted_iota(jnp.int32, slopes.shape, 1)
        for h in range(heads):
            slope = jnp.sum(jnp.where(lane == first + h, slopes_ref[...], 0.0), axis=1, keepdims=True)
            weights = jnp.where(causal, jnp.exp(-slope * distance), 0.0)
            out[h] = (weights / jnp.sum(weights, axis=-1, keepdims=True)).astype(BF16)

    carry = [(weight, False, 0, weight.shape[1])]
    return call(body, [shape((heads, length, length), BF16)], [slopes], held, carry=carry)


def flipped(array, axis, mask):
    return lax.ppermute(array, axis, [(i, i ^ mask) for i in range(lax.axis_size(axis))])


def on_device(parked, arriving, slot_table, value_weight, output_weight, slopes):
    sections, tensors, parts = (lax.axis_size(a) for a in ("section", "tensor", "dp"))
    slots, own, part_width = parked.shape[1:]
    width = part_width * parts
    half = output_weight.shape[1] // 2
    others = range(1, tensors)
    chips = range(2, parts, 2)
    bounds = [0, half // 2, half]
    chunks = [(a, b - a) for a, b in zip(bounds[:-1], bounds[1:], strict=True)]
    final = len(chunks) - 1

    def others_of(array):
        return [flipped(array, "tensor", t) for t in others]

    token, held = [None], []

    def run(kernel, first, *rest, **more):
        if token[0] is not None:
            if isinstance(first, list):
                first = [after(first[0], token[0]), *first[1:]]
            else:
                first = after(first, token[0])
        outs = kernel(first, *rest, held=held, **more)
        token[0] = outs[0]
        return outs

    upstream = [arriving[0]]
    pieces = [[a] for a in [upstream[0], *others_of(upstream[0])]]
    mixing, w_output = run(mixing_and_weight, slopes[None], output_weight[0], own * tensors, own)
    held.append(w_output)
    values = []
    for slot in range(slots):
        last = slot == slots - 1
        if slot > 0:
            upstream = [lax.ppermute(a, "section", [(i, i - 1) for i in range(1, sections)]) for a in upstream]
            pieces = [list(p) for p in zip(*[[a, *others_of(a)] for a in upstream], strict=True)]

        def product(j, other, received=None, carry=()):
            a, n = chunks[j]
            mixed = lambda first, *rest, held: grad_mixed_part([first, *pieces[1:]], *rest, held, carry)
            return run(mixed, pieces[0], w_output, other, a, n, received)

        halves, kept, across = [], [], []
        for j in range(len(chunks) + 1):
            if j <= final:
                halves.append(flipped(product(j, True)[0], "dp", 1))
            if j > 0:
                outs = product(j - 1, False, halves[j - 1])
                kept.append(outs[:2])
                if last and j == len(chunks):
                    normed = [after(a, outs[0]) for a in normed]
                    blocks = [b for a in normed for b in [a, *others_of(a)]]
                across.append([flipped(outs[1], "dp", m) for m in chips])
        if slot == 0:
            store = lax.ppermute(
                after(parked[0], kept[-1][1]), "section", [(i, sections - 1 - i) for i in range(sections)]
            )
        mine, theirs, total = [], [], None
        for j, (a, n) in enumerate(chunks):
            mine += run(unmix, kept[j][0], across[j], mixing, a // HEAD)
            theirs.append(flipped(mine[j], "dp", 1))
            for side, grads in enumerate((mine[j], theirs[j])):
                end = j == final and side == 1
                outs = run(grad_normed_part, grads, value_weight[0], side == 1, a, total, tensors if end else 0)
                if end:
                    keep, *sends = outs
                else:
                    total = outs[0]
        values.append([mine, theirs])
        received = [flipped(x, "tensor", t) for t, x in zip(others, sends, strict=True)]
        if slot == 0:
            inputs = run(ordered, store, slot_table.T)
        if last:
            held.clear()
            result = None
            todo = [(j, side) for j in range(len(chunks)) for side in range(2)]

            def write(j, side):
                terms = [v[side][j] for v in values]
                return run(value_grad_part, blocks, terms, result, value_weight.shape[1:], side == 1, chunks[j][0])[0]

            for piece in todo[: len(todo) * 3 // 4]:
                result = write(*piece)
        grad, sums = run(width_sums, keep, received, inputs, slot)
        sums, = run(added, sums, flipped(sums, "dp", 1))
        grad_stats = [sums] + [flipped(sums, "dp", m) for m in chips]
        if last:
            for piece in todo[len(todo) * 3 // 4 :]:
                result = write(*piece)
        if slot == 0:
            input_stats = grad_stats
        outs = run(finish, grad, upstream, inputs, slot, input_stats, grad_stats, width, 1)
        if slot == 0:
            normed = outs[-slots:]
            outs = outs[:-slots]
        upstream = outs

    return (upstream[0][None], result[None])


def solution(mesh):
    in_specs = (
        P("section", None, "tensor", "dp"),
        P("section", "tensor", "dp"),
        P(),
        P("section", "dp", "tensor"),
        P("section", "tensor", "dp"),
        P("tensor"),
    )
    out_specs = (P("section", "tensor", "dp"), P("section", "dp", "tensor"))
    return jax.shard_map(
        on_device, mesh=mesh, in_specs=in_specs, out_specs=out_specs, check_vma=False
    )
```

```python
import jax
import jax.numpy as jnp
from jax import lax
from jax.experimental import pallas as pl
from jax.experimental.pallas import tpu as pltpu
from jax.sharding import PartitionSpec as P

EPSILON = 1e-05
F32, BF16 = jnp.float32, jnp.bfloat16
NT = (((1,), (1,)), ((), ()))
TN = (((0,), (0,)), ((), ()))
SCOPED = 14 << 20
SMEM = pl.BlockSpec(memory_space=pltpu.SMEM)
VMEM = pl.BlockSpec(memory_space=pltpu.VMEM)
ANY = pl.BlockSpec(memory_space=pl.ANY)
HEAD = 128
COST = pl.CostEstimate(flops=8 * 10**9, bytes_accessed=10**8, transcendentals=0)
LIGHT = pl.CostEstimate(flops=1, bytes_accessed=1, transcendentals=0)


def call(body, outs, operands, first_spec=VMEM, light=False):
    return pl.pallas_call(
        body,
        in_specs=[first_spec] + [VMEM] * (len(operands) - 1),
        out_specs=[VMEM] * len(outs),
        out_shape=outs,
        compiler_params=pltpu.CompilerParams(vmem_limit_bytes=SCOPED),
        cost_estimate=LIGHT if light else COST,
    )(*operands)


def shape(dims, dtype):
    return jax.ShapeDtypeStruct(tuple(dims), dtype)


def after(array, *earlier):
    return lax.optimization_barrier((array, *earlier))[0]


def half_start(extent, other, offset):
    core = lax.axis_index("dp") % 2
    core = 1 - core if other else core
    return pl.multiple_of(core * (extent // 2) + offset, HEAD)


def grad_mixed_part(pieces, w_output, other, offset, size, received=None):
    counts = [len(p) for p in pieces]
    flat = [a for p in pieces for a in p]
    rows = sum(p[0].shape[0] for p in pieces)

    def body(*refs):
        blocks, at = [], 0
        for n in counts:
            blocks.append(jnp.concatenate([r[...] for r in refs[at : at + n]], axis=1))
            at += n
        ups = jnp.concatenate(blocks, axis=0)
        w = refs[at]
        start = half_start(w_output.shape[0], other, offset)
        part = lax.dot_general(ups, w[pl.ds(start, size), :], NT, preferred_element_type=F32)
        if other:
            refs[at + 1][...] = part.astype(BF16)
        else:
            part = part + refs[at + 1][...].astype(F32)
            refs[at + 2][...] = part
            refs[at + 3][...] = part.astype(BF16)

    if other:
        return call(body, [shape((rows, size), BF16)], [*flat, w_output])
    outs = [shape((rows, size), F32), shape((rows, size), BF16)]
    return call(body, outs, [*flat, w_output, received])


def unmix(kept, received, mixing, first_head):
    rows, size = kept.shape
    count = len(received)

    def body(*refs):
        mix, out = refs[count + 1], refs[count + 2]
        for h in range(size // HEAD):
            cols = slice(h * HEAD, (h + 1) * HEAD)
            total = refs[0][:, cols]
            for r in refs[1 : count + 1]:
                total = total + r[:, cols].astype(F32)
            out[:, cols] = lax.dot_general(
                mix[first_head + h], total.astype(BF16), TN, preferred_element_type=F32
            ).astype(BF16)

    return call(body, [shape((rows, size), BF16)], [kept, *received, mixing])


def grad_normed_part(grads, w_value, other, offset, total=None, pieces=0):
    (rows, size), width = grads.shape, w_value.shape[0]

    def body(v, w, *refs):
        start = half_start(w_value.shape[1], other, offset)
        sums = lax.dot_general(v[...], w[:, pl.ds(start, size)], NT, preferred_element_type=F32)
        if total is not None:
            sums = sums + refs[0][...]
        if not pieces:
            refs[-1][...] = sums
            return
        keep, *sends = refs[-pieces:]
        own = rows // pieces
        keep[...] = sums[:own]
        for t, ref in enumerate(sends):
            ref[...] = sums[(t + 1) * own : (t + 2) * own].astype(BF16)

    if pieces:
        outs = [shape((rows // pieces, width), F32)] + [shape((rows // pieces, width), BF16)] * (pieces - 1)
    else:
        outs = [shape((rows, width), F32)]
    operands = [grads, pltpu.with_memory_space_constraint(w_value, pltpu.VMEM)] + ([] if total is None else [total])
    return call(body, outs, operands)


def stacked(columns):
    rows = columns[0].shape[0]
    lane = lax.broadcasted_iota(jnp.int32, (rows, 128), 1)
    wide = jnp.zeros((rows, 128), F32)
    for k, column in enumerate(columns):
        wide = jnp.where(lane == k, column, wide)
    if rows % 128:
        wide = jnp.concatenate([wide, jnp.zeros((-rows % 128, 128), F32)], axis=0)
    return wide.T[:8]


def as_columns(stats, rows):
    return jnp.concatenate([stats, jnp.zeros((120, stats.shape[1]), F32)], axis=0).T[:rows]


def added(one, other):
    def body(a, b, out):
        out[...] = a[...] + b[...]

    return call(body, [shape(one.shape, one.dtype)], [one, other])


def ordered(store, table):
    slots = store.shape[0]

    def body(s, store_ref, *outs):
        section = lax.axis_index("section")
        for k, out in enumerate(outs):
            out[...] = store_ref[s[k, section]]

    return call(body, [shape(store.shape[1:], BF16)] * slots, [table, store], SMEM, light=True)


def width_sums(keep, received, inputs, slot):
    own, width = keep.shape
    slots = len(inputs)

    def body(keep_ref, *refs):
        ins, refs = refs[:slots], refs[slots:]
        grad_ref, stats = refs[-2:]
        grad = keep_ref[...]
        for r in refs[:-2]:
            grad = grad + r[...].astype(F32)
        grad_ref[...] = grad
        floats = [r[...].astype(F32) for r in ins]
        columns = [jnp.sum(grad, axis=1, keepdims=True), jnp.sum(grad * floats[slot], axis=1, keepdims=True)]
        if slot == 0:
            for x in floats:
                columns += [jnp.sum(x, axis=1, keepdims=True), jnp.sum(x * x, axis=1, keepdims=True)]
        stats[...] = stacked(columns)

    outs = [shape((own, width), F32), shape((8, -(-own // 128) * 128), F32)]
    return call(body, outs, [keep, *inputs, *received])


def finish(grad, upstream, inputs, slot, input_stats, grad_stats, width, parts):
    own, part = grad.shape
    slots = len(inputs)
    n_up, n_in, n_grad = len(upstream), len(input_stats), len(grad_stats)

    def body(grad_ref, *refs):
        x_refs, refs = refs[:slots], refs[slots:]
        ups, refs = refs[:n_up], refs[n_up:]
        ins, refs = refs[:n_in], refs[n_in:]
        grads, outs = refs[:n_grad], refs[n_grad:]
        total_in = ins[0][...]
        for r in ins[1:]:
            total_in = total_in + r[...]
        total = grads[0][...]
        for r in grads[1:]:
            total = total + r[...]
        in_columns = as_columns(total_in, own)
        columns = as_columns(total, own)

        def normal(k):
            center = in_columns[:, 2 * k + 2 : 2 * k + 3] / width
            inverse = lax.rsqrt(in_columns[:, 2 * k + 3 : 2 * k + 4] / width - center * center + EPSILON)
            return center, inverse, (x_refs[k][...].astype(F32) - center) * inverse

        center, inverse, scaled = normal(slot)
        first = columns[:, 0:1]
        second = (columns[:, 1:2] - center * first) * inverse
        above = jnp.concatenate([r[...] for r in ups], axis=1).astype(F32)
        made = (above + inverse * (grad_ref[...] - first / width - scaled * (second / width))).astype(BF16)
        for k in range(parts):
            outs[k][...] = made[:, k * (part // parts) : (k + 1) * (part // parts)]
        if slot == 0:
            for k in range(slots):
                outs[parts + k][...] = (scaled if k == slot else normal(k)[2]).astype(BF16)

    operands = [grad, *inputs, *upstream, *input_stats, *grad_stats]
    outs = [shape((own, part // parts), BF16)] * parts
    if slot == 0:
        outs += [shape((own, part), BF16)] * slots
    return call(body, outs, operands)


def value_grad_part(normed, grads, result, dims, other, offset):
    depth, width = sum(a.shape[0] for a in normed), normed[0].shape[1]
    blocks = len(normed)
    size = grads[0].shape[1]
    count = len(grads)
    block = 256 if width % 256 == 0 else 128
    steps = width // block
    given = [] if result is None else [result]

    def body(*refs):
        norms, refs = refs[:blocks], refs[blocks:]
        out, made, sems = refs[count + len(given) :]
        v = jnp.concatenate([r[...] for r in refs[:count]], axis=0)
        start = half_start(dims[1], other, offset)
        copies = []
        for i in range(steps):
            rows = pl.ds(i * block, block)
            made[rows, :] = lax.dot_general(
                jnp.concatenate([n[:, i * block : (i + 1) * block] for n in norms], axis=0),
                v,
                TN,
                preferred_element_type=F32,
            ).astype(BF16)
            copies.append(
                pltpu.make_async_copy(made.at[rows], out.at[rows, pl.ds(start, size)], sems.at[i])
            )
            copies[-1].start()
        for copy in copies:
            copy.wait()

    return pl.pallas_call(
        body,
        in_specs=[VMEM] * (blocks + count) + [ANY] * len(given),
        out_specs=[ANY],
        out_shape=[pltpu.HBM(dims, BF16)],
        scratch_shapes=[pltpu.VMEM((width, size), BF16), pltpu.SemaphoreType.DMA((steps,))],
        input_output_aliases={blocks + count: 0} if given else {},
        compiler_params=pltpu.CompilerParams(vmem_limit_bytes=SCOPED),
        cost_estimate=COST,
    )(*normed, *grads, *given)


def mixing_weights(slopes, length, own):
    heads = slopes.shape[1] // 2

    def body(slopes_ref, out):
        tensor = lax.axis_index("tensor")
        first = (lax.axis_index("dp") % 2) * heads

        def place(dim):
            local = lax.broadcasted_iota(jnp.int32, (length, length), dim)
            return ((local // own) ^ tensor) * own + local % own

        distance = (place(0) - place(1)).astype(F32)
        causal = distance >= 0
        distance = jnp.where(causal, distance, 0.0)
        lane = lax.broadcasted_iota(jnp.int32, slopes.shape, 1)
        for h in range(heads):
            slope = jnp.sum(jnp.where(lane == first + h, slopes_ref[...], 0.0), axis=1, keepdims=True)
            weights = jnp.where(causal, jnp.exp(-slope * distance), 0.0)
            out[h] = (weights / jnp.sum(weights, axis=-1, keepdims=True)).astype(BF16)

    return call(body, [shape((heads, length, length), BF16)], [slopes])


def flipped(array, axis, mask):
    return lax.ppermute(array, axis, [(i, i ^ mask) for i in range(lax.axis_size(axis))])


def on_device(parked, arriving, slot_table, value_weight, output_weight, slopes):
    sections, tensors, parts = (lax.axis_size(a) for a in ("section", "tensor", "dp"))
    slots, own, part_width = parked.shape[1:]
    width = part_width * parts
    half = output_weight.shape[1] // 2
    others = range(1, tensors)
    chips = range(2, parts, 2)
    bounds = [0, half // 2, half]
    chunks = [(a, b - a) for a, b in zip(bounds[:-1], bounds[1:], strict=True)]
    final = len(chunks) - 1

    def others_of(array):
        return [flipped(array, "tensor", t) for t in others]

    token = [None]

    def run(kernel, first, *rest):
        if token[0] is not None:
            if isinstance(first, list):
                first = [after(first[0], token[0]), *first[1:]]
            else:
                first = after(first, token[0])
        outs = kernel(first, *rest)
        token[0] = outs[0]
        return outs

    upstream = [arriving[0]]
    pieces = [[a] for a in [upstream[0], *others_of(upstream[0])]]
    mixing, = run(mixing_weights, slopes[None], own * tensors, own)
    pieces[0][0] = after(pieces[0][0], mixing)
    w_output = pltpu.with_memory_space_constraint(output_weight[0], pltpu.VMEM)
    values = []
    for slot in range(slots):
        last = slot == slots - 1
        if slot > 0:
            pieces = [
                [
                    lax.ppermute(
                        upstream[0],
                        ("section", "tensor"),
                        [(i * tensors + k, (i - 1) * tensors + (k ^ t)) for i in range(1, sections) for k in range(tensors)],
                    )
                ]
                for t in range(tensors)
            ]
            upstream = pieces[0]

        def product(j, other, received=None):
            a, n = chunks[j]
            mixed = lambda first, *rest: grad_mixed_part([first, *pieces[1:]], *rest)
            return run(mixed, pieces[0], w_output, other, a, n, received)

        halves, kept, across = [], [], []
        for j in range(len(chunks) + 1):
            if j <= final:
                halves.append(flipped(product(j, True)[0], "dp", 1))
            if j > 0:
                outs = product(j - 1, False, halves[j - 1])
                kept.append(outs[:2])
                if last and j == len(chunks):
                    normed = [after(a, outs[0]) for a in normed]
                    blocks = [b for a in normed for b in [a, *others_of(a)]]
                across.append([flipped(outs[1], "dp", m) for m in chips])
        if slot == 0:
            store = lax.ppermute(
                after(parked[0], kept[-1][1]), "section", [(i, sections - 1 - i) for i in range(sections)]
            )
        mine, theirs, total = [], [], None
        for j, (a, n) in enumerate(chunks):
            mine += run(unmix, kept[j][0], across[j], mixing, a // HEAD)
            theirs.append(flipped(mine[j], "dp", 1))
            for side, grads in enumerate((mine[j], theirs[j])):
                end = j == final and side == 1
                outs = run(grad_normed_part, grads, value_weight[0], side == 1, a, total, tensors if end else 0)
                if end:
                    keep, *sends = outs
                else:
                    total = outs[0]
        values.append([mine, theirs])
        received = [flipped(x, "tensor", t) for t, x in zip(others, sends, strict=True)]
        if slot == 0:
            inputs = run(ordered, store, slot_table.T)
        if last:
            result = None
            todo = [(j, side) for j in range(len(chunks)) for side in range(2)]

            def write(j, side):
                terms = [v[side][j] for v in values]
                return run(value_grad_part, blocks, terms, result, value_weight.shape[1:], side == 1, chunks[j][0])[0]

            for piece in todo[: len(todo) * 3 // 4]:
                result = write(*piece)
        grad, sums = run(width_sums, keep, received, inputs, slot)
        sums, = run(added, sums, flipped(sums, "dp", 1))
        grad_stats = [sums] + [flipped(sums, "dp", m) for m in chips]
        if last:
            for piece in todo[len(todo) * 3 // 4 :]:
                result = write(*piece)
        if slot == 0:
            input_stats = grad_stats
        outs = run(finish, grad, upstream, inputs, slot, input_stats, grad_stats, width, 1)
        if slot == 0:
            normed = outs[-slots:]
            outs = outs[:-slots]
        upstream = outs

    return (upstream[0][None], result[None])


def solution(mesh):
    in_specs = (
        P("section", None, "tensor", "dp"),
        P("section", "tensor", "dp"),
        P(),
        P("section", "dp", "tensor"),
        P("section", "tensor", "dp"),
        P("tensor"),
    )
    out_specs = (P("section", "tensor", "dp"), P("section", "dp", "tensor"))
    return jax.shard_map(
        on_device, mesh=mesh, in_specs=in_specs, out_specs=out_specs, check_vma=False
    )
```

```python
import jax
import jax.numpy as jnp
from jax import lax
from jax.experimental import pallas as pl
from jax.experimental.pallas import tpu as pltpu
from jax.sharding import PartitionSpec as P

EPSILON = 1e-05
F32, BF16 = jnp.float32, jnp.bfloat16
NT = (((1,), (1,)), ((), ()))
TN = (((0,), (0,)), ((), ()))
SCOPED = 14 << 20
SMEM = pl.BlockSpec(memory_space=pltpu.SMEM)
VMEM = pl.BlockSpec(memory_space=pltpu.VMEM)
ANY = pl.BlockSpec(memory_space=pl.ANY)
HEAD = 128
COST = pl.CostEstimate(flops=8 * 10**9, bytes_accessed=10**8, transcendentals=0)
LIGHT = pl.CostEstimate(flops=1, bytes_accessed=1, transcendentals=0)


def call(body, outs, operands, first_spec=VMEM, light=False):
    return pl.pallas_call(
        body,
        in_specs=[first_spec] + [VMEM] * (len(operands) - 1),
        out_specs=[VMEM] * len(outs),
        out_shape=outs,
        compiler_params=pltpu.CompilerParams(vmem_limit_bytes=SCOPED),
        cost_estimate=LIGHT if light else COST,
    )(*operands)


def shape(dims, dtype):
    return jax.ShapeDtypeStruct(tuple(dims), dtype)


def after(array, *earlier):
    return lax.optimization_barrier((array, *earlier))[0]


def half_start(extent, other, offset):
    core = lax.axis_index("dp") % 2
    core = 1 - core if other else core
    return pl.multiple_of(core * (extent // 2) + offset, HEAD)


def grad_mixed_part(pieces, w_output, other, offset, size, received=None):
    counts = [len(p) for p in pieces]
    flat = [a for p in pieces for a in p]
    rows = sum(p[0].shape[0] for p in pieces)

    def body(*refs):
        blocks, at = [], 0
        for n in counts:
            blocks.append(jnp.concatenate([r[...] for r in refs[at : at + n]], axis=1))
            at += n
        ups = jnp.concatenate(blocks, axis=0)
        w = refs[at]
        start = half_start(w_output.shape[0], other, offset)
        part = lax.dot_general(ups, w[pl.ds(start, size), :], NT, preferred_element_type=F32)
        if other:
            refs[at + 1][...] = part.astype(BF16)
        else:
            part = part + refs[at + 1][...].astype(F32)
            refs[at + 2][...] = part
            refs[at + 3][...] = part.astype(BF16)

    if other:
        return call(body, [shape((rows, size), BF16)], [*flat, w_output])
    outs = [shape((rows, size), F32), shape((rows, size), BF16)]
    return call(body, outs, [*flat, w_output, received])


def unmix(kept, received, mixing, first_head):
    rows, size = kept.shape
    count = len(received)

    def body(*refs):
        mix, out = refs[count + 1], refs[count + 2]
        for h in range(size // HEAD):
            cols = slice(h * HEAD, (h + 1) * HEAD)
            total = refs[0][:, cols]
            for r in refs[1 : count + 1]:
                total = total + r[:, cols].astype(F32)
            out[:, cols] = lax.dot_general(
                mix[first_head + h], total.astype(BF16), TN, preferred_element_type=F32
            ).astype(BF16)

    return call(body, [shape((rows, size), BF16)], [kept, *received, mixing])


def grad_normed_part(grads, w_value, other, offset, total=None, pieces=0):
    (rows, size), width = grads.shape, w_value.shape[0]

    def body(v, w, *refs):
        start = half_start(w_value.shape[1], other, offset)
        sums = lax.dot_general(v[...], w[:, pl.ds(start, size)], NT, preferred_element_type=F32)
        if total is not None:
            sums = sums + refs[0][...]
        if not pieces:
            refs[-1][...] = sums
            return
        keep, *sends = refs[-pieces:]
        own = rows // pieces
        keep[...] = sums[:own]
        for t, ref in enumerate(sends):
            ref[...] = sums[(t + 1) * own : (t + 2) * own].astype(BF16)

    if pieces:
        outs = [shape((rows // pieces, width), F32)] + [shape((rows // pieces, width), BF16)] * (pieces - 1)
    else:
        outs = [shape((rows, width), F32)]
    operands = [grads, pltpu.with_memory_space_constraint(w_value, pltpu.VMEM)] + ([] if total is None else [total])
    return call(body, outs, operands)


def stacked(columns):
    rows = columns[0].shape[0]
    lane = lax.broadcasted_iota(jnp.int32, (rows, 128), 1)
    wide = jnp.zeros((rows, 128), F32)
    for k, column in enumerate(columns):
        wide = jnp.where(lane == k, column, wide)
    if rows % 128:
        wide = jnp.concatenate([wide, jnp.zeros((-rows % 128, 128), F32)], axis=0)
    return wide.T[:8]


def as_columns(stats, rows):
    return jnp.concatenate([stats, jnp.zeros((120, stats.shape[1]), F32)], axis=0).T[:rows]


def ordered(store, table):
    slots = store.shape[0]

    def body(s, store_ref, *outs):
        section = lax.axis_index("section")
        for k, out in enumerate(outs):
            out[...] = store_ref[s[k, section]]

    return call(body, [shape(store.shape[1:], BF16)] * slots, [table, store], SMEM, light=True)


def width_sums(keep, received, inputs, slot):
    own, width = keep.shape
    slots = len(inputs)

    def body(keep_ref, *refs):
        ins, refs = refs[:slots], refs[slots:]
        grad_ref, stats = refs[-2:]
        grad = keep_ref[...]
        for r in refs[:-2]:
            grad = grad + r[...].astype(F32)
        grad_ref[...] = grad
        floats = [r[...].astype(F32) for r in ins]
        columns = [jnp.sum(grad, axis=1, keepdims=True), jnp.sum(grad * floats[slot], axis=1, keepdims=True)]
        if slot == 0:
            for x in floats:
                columns += [jnp.sum(x, axis=1, keepdims=True), jnp.sum(x * x, axis=1, keepdims=True)]
        stats[...] = stacked(columns)

    outs = [shape((own, width), F32), shape((8, -(-own // 128) * 128), F32)]
    return call(body, outs, [keep, *inputs, *received])


def finish(grad, upstream, inputs, slot, input_stats, grad_stats, width, parts):
    own, part = grad.shape
    slots = len(inputs)
    n_up, n_in, n_grad = len(upstream), len(input_stats), len(grad_stats)

    def body(grad_ref, *refs):
        x_refs, refs = refs[:slots], refs[slots:]
        ups, refs = refs[:n_up], refs[n_up:]
        ins, refs = refs[:n_in], refs[n_in:]
        grads, outs = refs[:n_grad], refs[n_grad:]
        total_in = ins[0][...]
        for r in ins[1:]:
            total_in = total_in + r[...]
        total = grads[0][...]
        for r in grads[1:]:
            total = total + r[...]
        in_columns = as_columns(total_in, own)
        columns = as_columns(total, own)

        def normal(k):
            center = in_columns[:, 2 * k + 2 : 2 * k + 3] / width
            inverse = lax.rsqrt(in_columns[:, 2 * k + 3 : 2 * k + 4] / width - center * center + EPSILON)
            return center, inverse, (x_refs[k][...].astype(F32) - center) * inverse

        center, inverse, scaled = normal(slot)
        first = columns[:, 0:1]
        second = (columns[:, 1:2] - center * first) * inverse
        above = jnp.concatenate([r[...] for r in ups], axis=1).astype(F32)
        made = (above + inverse * (grad_ref[...] - first / width - scaled * (second / width))).astype(BF16)
        for k in range(parts):
            outs[k][...] = made[:, k * (part // parts) : (k + 1) * (part // parts)]
        if slot == 0:
            for k in range(slots):
                outs[parts + k][...] = (scaled if k == slot else normal(k)[2]).astype(BF16)

    operands = [grad, *inputs, *upstream, *input_stats, *grad_stats]
    outs = [shape((own, part // parts), BF16)] * parts
    if slot == 0:
        outs += [shape((own, part), BF16)] * slots
    return call(body, outs, operands)


def value_grad(normed, terms, dims):
    depth, width = sum(a.shape[0] for a in normed), normed[0].shape[1]
    blocks, count = len(normed), len(terms)
    slots, size = len(terms[0][0]), terms[0][0][0].shape[1]
    block = 256 if width % 256 == 0 else 128
    steps = width // block

    def body(*refs):
        norms, refs = refs[:blocks], refs[blocks:]
        grads, refs = refs[: count * slots], refs[count * slots :]
        out, made, sems = refs
        copies = []
        for k, (_, other, offset) in enumerate(terms):
            v = jnp.concatenate([r[...] for r in grads[k * slots : (k + 1) * slots]], axis=0)
            start = half_start(dims[1], other, offset)
            for i in range(steps):
                rows = pl.ds(i * block, block)
                made[k, rows, :] = lax.dot_general(
                    jnp.concatenate([n[:, i * block : (i + 1) * block] for n in norms], axis=0),
                    v,
                    TN,
                    preferred_element_type=F32,
                ).astype(BF16)
                copies.append(
                    pltpu.make_async_copy(
                        made.at[k, rows], out.at[rows, pl.ds(start, size)], sems.at[k, i]
                    )
                )
                copies[-1].start()
        for copy in copies:
            copy.wait()

    flat = [g for grads, _, _ in terms for g in grads]
    return pl.pallas_call(
        body,
        in_specs=[VMEM] * (blocks + len(flat)),
        out_specs=[ANY],
        out_shape=[pltpu.HBM(dims, BF16)],
        scratch_shapes=[pltpu.VMEM((count, width, size), BF16), pltpu.SemaphoreType.DMA((count, steps))],
        compiler_params=pltpu.CompilerParams(vmem_limit_bytes=SCOPED),
        cost_estimate=COST,
    )(*normed, *flat)


def mixing_weights(slopes, length, own):
    heads = slopes.shape[1] // 2

    def body(slopes_ref, out):
        tensor = lax.axis_index("tensor")
        first = (lax.axis_index("dp") % 2) * heads

        def place(dim):
            local = lax.broadcasted_iota(jnp.int32, (length, length), dim)
            return ((local // own) ^ tensor) * own + local % own

        distance = (place(0) - place(1)).astype(F32)
        causal = distance >= 0
        distance = jnp.where(causal, distance, 0.0)
        lane = lax.broadcasted_iota(jnp.int32, slopes.shape, 1)
        for h in range(heads):
            slope = jnp.sum(jnp.where(lane == first + h, slopes_ref[...], 0.0), axis=1, keepdims=True)
            weights = jnp.where(causal, jnp.exp(-slope * distance), 0.0)
            out[h] = (weights / jnp.sum(weights, axis=-1, keepdims=True)).astype(BF16)

    return call(body, [shape((heads, length, length), BF16)], [slopes])


def flipped(array, axis, mask):
    return lax.ppermute(array, axis, [(i, i ^ mask) for i in range(lax.axis_size(axis))])


def on_device(parked, arriving, slot_table, value_weight, output_weight, slopes):
    sections, tensors, parts = (lax.axis_size(a) for a in ("section", "tensor", "dp"))
    slots, own, part_width = parked.shape[1:]
    width = part_width * parts
    half = output_weight.shape[1] // 2
    others = range(1, tensors)
    chips = range(2, parts, 2)
    bounds = [0, half // 2, half]
    chunks = [(a, b - a) for a, b in zip(bounds[:-1], bounds[1:], strict=True)]
    final = len(chunks) - 1

    def others_of(array):
        return [flipped(array, "tensor", t) for t in others]

    token = [None]

    def run(kernel, first, *rest):
        if token[0] is not None:
            if isinstance(first, list):
                first = [after(first[0], token[0]), *first[1:]]
            else:
                first = after(first, token[0])
        outs = kernel(first, *rest)
        token[0] = outs[0]
        return outs

    upstream = [arriving[0]]
    pieces = [[a] for a in [upstream[0], *others_of(upstream[0])]]
    mixing, = run(mixing_weights, slopes[None], own * tensors, own)
    pieces[0][0] = after(pieces[0][0], mixing)
    w_output = pltpu.with_memory_space_constraint(output_weight[0], pltpu.VMEM)
    values = []
    for slot in range(slots):
        last = slot == slots - 1
        if slot > 0:
            pieces = [
                [
                    lax.ppermute(
                        upstream[0],
                        ("section", "tensor"),
                        [(i * tensors + k, (i - 1) * tensors + (k ^ t)) for i in range(1, sections) for k in range(tensors)],
                    )
                ]
                for t in range(tensors)
            ]
            upstream = pieces[0]

        def product(j, other, received=None):
            a, n = chunks[j]
            mixed = lambda first, *rest: grad_mixed_part([first, *pieces[1:]], *rest)
            return run(mixed, pieces[0], w_output, other, a, n, received)

        halves, kept, across = [], [], []
        for j in range(len(chunks) + 1):
            if j <= final:
                halves.append(flipped(product(j, True)[0], "dp", 1))
            if j > 0:
                outs = product(j - 1, False, halves[j - 1])
                kept.append(outs[:2])
                if last and j == len(chunks):
                    normed = [after(a, outs[0]) for a in normed]
                    blocks = [b for a in normed for b in [a, *others_of(a)]]
                across.append([flipped(outs[1], "dp", m) for m in chips])
        if slot == 0:
            store = lax.ppermute(
                after(parked[0], kept[-1][1]), "section", [(i, sections - 1 - i) for i in range(sections)]
            )
        mine, theirs, total = [], [], None
        for j, (a, n) in enumerate(chunks):
            mine += run(unmix, kept[j][0], across[j], mixing, a // HEAD)
            theirs.append(flipped(mine[j], "dp", 1))
            for side, grads in enumerate((mine[j], theirs[j])):
                end = j == final and side == 1
                outs = run(grad_normed_part, grads, value_weight[0], side == 1, a, total, tensors if end else 0)
                if end:
                    keep, *sends = outs
                else:
                    total = outs[0]
        values.append([mine, theirs])
        received = [flipped(x, "tensor", t) for t, x in zip(others, sends, strict=True)]
        if slot == 0:
            inputs = run(ordered, store, slot_table.T)
        if last:
            terms = [
                ([v[side][j] for v in values], side == 1, a) for j, (a, _) in enumerate(chunks) for side in range(2)
            ]
            result, = run(value_grad, blocks, terms, value_weight.shape[1:])
        grad, sums = run(width_sums, keep, received, inputs, slot)
        grad_stats = [sums] + [flipped(sums, "dp", m) for m in range(1, parts)]
        if slot == 0:
            input_stats = grad_stats
        outs = run(finish, grad, upstream, inputs, slot, input_stats, grad_stats, width, 1)
        if slot == 0:
            normed = outs[-slots:]
            outs = outs[:-slots]
        upstream = outs

    return (upstream[0][None], result[None])


def solution(mesh):
    in_specs = (
        P("section", None, "tensor", "dp"),
        P("section", "tensor", "dp"),
        P(),
        P("section", "dp", "tensor"),
        P("section", "tensor", "dp"),
        P("tensor"),
    )
    out_specs = (P("section", "tensor", "dp"), P("section", "dp", "tensor"))
    return jax.shard_map(
        on_device, mesh=mesh, in_specs=in_specs, out_specs=out_specs, check_vma=False
    )
```

```python
import jax
import jax.numpy as jnp
from jax import lax
from jax.experimental import pallas as pl
from jax.experimental.pallas import tpu as pltpu
from jax.sharding import PartitionSpec as P

EPSILON = 1e-05
F32, BF16 = jnp.float32, jnp.bfloat16
NT = (((1,), (1,)), ((), ()))
TN = (((0,), (0,)), ((), ()))
SCOPED = 14 << 20
SMEM = pl.BlockSpec(memory_space=pltpu.SMEM)
VMEM = pl.BlockSpec(memory_space=pltpu.VMEM)
ANY = pl.BlockSpec(memory_space=pl.ANY)
HEAD = 128
COST = pl.CostEstimate(flops=8 * 10**9, bytes_accessed=10**8, transcendentals=0)
LIGHT = pl.CostEstimate(flops=1, bytes_accessed=1, transcendentals=0)


def call(body, outs, operands, first_spec=VMEM, light=False):
    return pl.pallas_call(
        body,
        in_specs=[first_spec] + [VMEM] * (len(operands) - 1),
        out_specs=[VMEM] * len(outs),
        out_shape=outs,
        compiler_params=pltpu.CompilerParams(vmem_limit_bytes=SCOPED),
        cost_estimate=LIGHT if light else COST,
    )(*operands)


def shape(dims, dtype):
    return jax.ShapeDtypeStruct(tuple(dims), dtype)


def after(array, *earlier):
    return lax.optimization_barrier((array, *earlier))[0]


def half_start(extent, other, offset):
    core = lax.axis_index("dp") % 2
    core = 1 - core if other else core
    return pl.multiple_of(core * (extent // 2) + offset, HEAD)


def grad_mixed_part(pieces, w_output, other, offset, size, received=None):
    counts = [len(p) for p in pieces]
    flat = [a for p in pieces for a in p]
    rows = sum(p[0].shape[0] for p in pieces)

    def body(*refs):
        blocks, at = [], 0
        for n in counts:
            blocks.append(jnp.concatenate([r[...] for r in refs[at : at + n]], axis=1))
            at += n
        ups = jnp.concatenate(blocks, axis=0)
        w = refs[at]
        start = half_start(w_output.shape[0], other, offset)
        part = lax.dot_general(ups, w[pl.ds(start, size), :], NT, preferred_element_type=F32)
        if other:
            refs[at + 1][...] = part.astype(BF16)
        else:
            part = part + refs[at + 1][...].astype(F32)
            refs[at + 2][...] = part
            refs[at + 3][...] = part.astype(BF16)

    if other:
        return call(body, [shape((rows, size), BF16)], [*flat, w_output])
    outs = [shape((rows, size), F32), shape((rows, size), BF16)]
    return call(body, outs, [*flat, w_output, received])


def unmix(kept, received, mixing, first_head):
    rows, size = kept.shape
    count = len(received)

    def body(*refs):
        mix, out = refs[count + 1], refs[count + 2]
        for h in range(size // HEAD):
            cols = slice(h * HEAD, (h + 1) * HEAD)
            total = refs[0][:, cols]
            for r in refs[1 : count + 1]:
                total = total + r[:, cols].astype(F32)
            out[:, cols] = lax.dot_general(
                mix[first_head + h], total.astype(BF16), TN, preferred_element_type=F32
            ).astype(BF16)

    return call(body, [shape((rows, size), BF16)], [kept, *received, mixing])


def grad_normed_part(grads, w_value, other, offset, total=None, pieces=0):
    (rows, size), width = grads.shape, w_value.shape[0]

    def body(v, w, *refs):
        start = half_start(w_value.shape[1], other, offset)
        sums = lax.dot_general(v[...], w[:, pl.ds(start, size)], NT, preferred_element_type=F32)
        if total is not None:
            sums = sums + refs[0][...]
        if not pieces:
            refs[-1][...] = sums
            return
        keep, *sends = refs[-pieces:]
        own = rows // pieces
        keep[...] = sums[:own]
        for t, ref in enumerate(sends):
            ref[...] = sums[(t + 1) * own : (t + 2) * own].astype(BF16)

    if pieces:
        outs = [shape((rows // pieces, width), F32)] + [shape((rows // pieces, width), BF16)] * (pieces - 1)
    else:
        outs = [shape((rows, width), F32)]
    operands = [grads, pltpu.with_memory_space_constraint(w_value, pltpu.VMEM)] + ([] if total is None else [total])
    return call(body, outs, operands)


def stacked(columns):
    rows = columns[0].shape[0]
    lane = lax.broadcasted_iota(jnp.int32, (rows, 128), 1)
    wide = jnp.zeros((rows, 128), F32)
    for k, column in enumerate(columns):
        wide = jnp.where(lane == k, column, wide)
    if rows % 128:
        wide = jnp.concatenate([wide, jnp.zeros((-rows % 128, 128), F32)], axis=0)
    return wide.T[:8]


def as_columns(stats, rows):
    return jnp.concatenate([stats, jnp.zeros((120, stats.shape[1]), F32)], axis=0).T[:rows]


def ordered(store, table):
    slots = store.shape[0]

    def body(s, store_ref, *outs):
        section = lax.axis_index("section")
        for k, out in enumerate(outs):
            out[...] = store_ref[s[k, section]]

    return call(body, [shape(store.shape[1:], BF16)] * slots, [table, store], SMEM, light=True)


def width_sums(keep, received, inputs, slot):
    own, width = keep.shape
    slots = len(inputs)

    def body(keep_ref, *refs):
        ins, refs = refs[:slots], refs[slots:]
        grad_ref, stats = refs[-2:]
        grad = keep_ref[...]
        for r in refs[:-2]:
            grad = grad + r[...].astype(F32)
        grad_ref[...] = grad
        floats = [r[...].astype(F32) for r in ins]
        columns = [jnp.sum(grad, axis=1, keepdims=True), jnp.sum(grad * floats[slot], axis=1, keepdims=True)]
        if slot == 0:
            for x in floats:
                columns += [jnp.sum(x, axis=1, keepdims=True), jnp.sum(x * x, axis=1, keepdims=True)]
        stats[...] = stacked(columns)

    outs = [shape((own, width), F32), shape((8, -(-own // 128) * 128), F32)]
    return call(body, outs, [keep, *inputs, *received])


def finish(grad, upstream, inputs, slot, input_stats, grad_stats, width, parts):
    own, part = grad.shape
    slots = len(inputs)
    n_up, n_in, n_grad = len(upstream), len(input_stats), len(grad_stats)

    def body(grad_ref, *refs):
        x_refs, refs = refs[:slots], refs[slots:]
        ups, refs = refs[:n_up], refs[n_up:]
        ins, refs = refs[:n_in], refs[n_in:]
        grads, outs = refs[:n_grad], refs[n_grad:]
        total_in = ins[0][...]
        for r in ins[1:]:
            total_in = total_in + r[...]
        total = grads[0][...]
        for r in grads[1:]:
            total = total + r[...]
        in_columns = as_columns(total_in, own)
        columns = as_columns(total, own)

        def normal(k):
            center = in_columns[:, 2 * k + 2 : 2 * k + 3] / width
            inverse = lax.rsqrt(in_columns[:, 2 * k + 3 : 2 * k + 4] / width - center * center + EPSILON)
            return center, inverse, (x_refs[k][...].astype(F32) - center) * inverse

        center, inverse, scaled = normal(slot)
        first = columns[:, 0:1]
        second = (columns[:, 1:2] - center * first) * inverse
        above = jnp.concatenate([r[...] for r in ups], axis=1).astype(F32)
        made = (above + inverse * (grad_ref[...] - first / width - scaled * (second / width))).astype(BF16)
        for k in range(parts):
            outs[k][...] = made[:, k * (part // parts) : (k + 1) * (part // parts)]
        if slot == 0:
            for k in range(slots):
                outs[parts + k][...] = (scaled if k == slot else normal(k)[2]).astype(BF16)

    operands = [grad, *inputs, *upstream, *input_stats, *grad_stats]
    outs = [shape((own, part // parts), BF16)] * parts
    if slot == 0:
        outs += [shape((own, part), BF16)] * slots
    return call(body, outs, operands)


def value_grad(normed, terms, dims):
    depth, width = sum(a.shape[0] for a in normed), normed[0].shape[1]
    blocks, count = len(normed), len(terms)
    slots, size = len(terms[0][0]), terms[0][0][0].shape[1]
    block = 256 if width % 256 == 0 else 128
    steps = width // block

    def body(*refs):
        norms, refs = refs[:blocks], refs[blocks:]
        grads, refs = refs[: count * slots], refs[count * slots :]
        out, made, sems = refs
        copies = []
        for k, (_, other, offset) in enumerate(terms):
            v = jnp.concatenate([r[...] for r in grads[k * slots : (k + 1) * slots]], axis=0)
            start = half_start(dims[1], other, offset)
            for i in range(steps):
                rows = pl.ds(i * block, block)
                made[k, rows, :] = lax.dot_general(
                    jnp.concatenate([n[:, i * block : (i + 1) * block] for n in norms], axis=0),
                    v,
                    TN,
                    preferred_element_type=F32,
                ).astype(BF16)
                copies.append(
                    pltpu.make_async_copy(
                        made.at[k, rows], out.at[rows, pl.ds(start, size)], sems.at[k, i]
                    )
                )
                copies[-1].start()
        for copy in copies:
            copy.wait()

    flat = [g for grads, _, _ in terms for g in grads]
    return pl.pallas_call(
        body,
        in_specs=[VMEM] * (blocks + len(flat)),
        out_specs=[ANY],
        out_shape=[pltpu.HBM(dims, BF16)],
        scratch_shapes=[pltpu.VMEM((count, width, size), BF16), pltpu.SemaphoreType.DMA((count, steps))],
        compiler_params=pltpu.CompilerParams(vmem_limit_bytes=SCOPED),
        cost_estimate=COST,
    )(*normed, *flat)


def mixing_weights(slopes, length, own):
    heads = slopes.shape[1] // 2

    def body(slopes_ref, out):
        tensor = lax.axis_index("tensor")
        first = (lax.axis_index("dp") % 2) * heads

        def place(dim):
            local = lax.broadcasted_iota(jnp.int32, (length, length), dim)
            return ((local // own) ^ tensor) * own + local % own

        distance = (place(0) - place(1)).astype(F32)
        causal = distance >= 0
        distance = jnp.where(causal, distance, 0.0)
        lane = lax.broadcasted_iota(jnp.int32, slopes.shape, 1)
        for h in range(heads):
            slope = jnp.sum(jnp.where(lane == first + h, slopes_ref[...], 0.0), axis=1, keepdims=True)
            weights = jnp.where(causal, jnp.exp(-slope * distance), 0.0)
            out[h] = (weights / jnp.sum(weights, axis=-1, keepdims=True)).astype(BF16)

    return call(body, [shape((heads, length, length), BF16)], [slopes])


def flipped(array, axis, mask):
    return lax.ppermute(array, axis, [(i, i ^ mask) for i in range(lax.axis_size(axis))])


def on_device(parked, arriving, slot_table, value_weight, output_weight, slopes):
    sections, tensors, parts = (lax.axis_size(a) for a in ("section", "tensor", "dp"))
    slots, own, part_width = parked.shape[1:]
    width = part_width * parts
    half = output_weight.shape[1] // 2
    others = range(1, tensors)
    chips = range(2, parts, 2)
    bounds = [0, half // 2, half]
    chunks = [(a, b - a) for a, b in zip(bounds[:-1], bounds[1:], strict=True)]
    final = len(chunks) - 1

    def others_of(array):
        return [flipped(array, "tensor", t) for t in others]

    token = [None]

    def run(kernel, first, *rest):
        if token[0] is not None:
            if isinstance(first, list):
                first = [after(first[0], token[0]), *first[1:]]
            else:
                first = after(first, token[0])
        outs = kernel(first, *rest)
        token[0] = outs[0]
        return outs

    upstream = [arriving[0]]
    pieces = [[a] for a in [upstream[0], *others_of(upstream[0])]]
    mixing, = run(mixing_weights, slopes[None], own * tensors, own)
    pieces[0][0] = after(pieces[0][0], mixing)
    w_output = pltpu.with_memory_space_constraint(output_weight[0], pltpu.VMEM)
    values = []
    for slot in range(slots):
        last = slot == slots - 1
        if slot > 0:
            def from_above(array, t):
                return lax.ppermute(
                    array,
                    ("section", "tensor"),
                    [(i * tensors + k, (i - 1) * tensors + (k ^ t)) for i in range(1, sections) for k in range(tensors)],
                )

            above, upstream = upstream, [from_above(a, 0) for a in upstream]
            pieces = [upstream] + [[from_above(above[0], t), *(flipped(a, "tensor", t) for a in upstream[1:])] for t in others]

        def product(j, other, received=None):
            a, n = chunks[j]
            mixed = lambda first, *rest: grad_mixed_part([first, *pieces[1:]], *rest)
            return run(mixed, pieces[0], w_output, other, a, n, received)

        halves, kept, across = [], [], []
        for j in range(len(chunks) + 1):
            if j <= final:
                halves.append(flipped(product(j, True)[0], "dp", 1))
            if j > 0:
                outs = product(j - 1, False, halves[j - 1])
                kept.append(outs[:2])
                if last and j == len(chunks):
                    normed = [after(a, outs[0]) for a in normed]
                    blocks = [b for a in normed for b in [a, *others_of(a)]]
                across.append([flipped(outs[1], "dp", m) for m in chips])
        if slot == 0:
            store = lax.ppermute(
                after(parked[0], kept[-1][1]), "section", [(i, sections - 1 - i) for i in range(sections)]
            )
        mine, theirs, total = [], [], None
        for j, (a, n) in enumerate(chunks):
            mine += run(unmix, kept[j][0], across[j], mixing, a // HEAD)
            theirs.append(flipped(mine[j], "dp", 1))
            for side, grads in enumerate((mine[j], theirs[j])):
                end = j == final and side == 1
                outs = run(grad_normed_part, grads, value_weight[0], side == 1, a, total, tensors if end else 0)
                if end:
                    keep, *sends = outs
                else:
                    total = outs[0]
        values.append([mine, theirs])
        received = [flipped(x, "tensor", t) for t, x in zip(others, sends, strict=True)]
        if slot == 0:
            inputs = run(ordered, store, slot_table.T)
        if last:
            terms = [
                ([v[side][j] for v in values], side == 1, a) for j, (a, _) in enumerate(chunks) for side in range(2)
            ]
            result, = run(value_grad, blocks, terms, value_weight.shape[1:])
        grad, sums = run(width_sums, keep, received, inputs, slot)
        grad_stats = [sums] + [flipped(sums, "dp", m) for m in range(1, parts)]
        if slot == 0:
            input_stats = grad_stats
        outs = run(finish, grad, upstream, inputs, slot, input_stats, grad_stats, width, 1 if last else 2)
        if slot == 0:
            normed = outs[-slots:]
            outs = outs[:-slots]
        upstream = outs

    return (upstream[0][None], result[None])


def solution(mesh):
    in_specs = (
        P("section", None, "tensor", "dp"),
        P("section", "tensor", "dp"),
        P(),
        P("section", "dp", "tensor"),
        P("section", "tensor", "dp"),
        P("tensor"),
    )
    out_specs = (P("section", "tensor", "dp"), P("section", "dp", "tensor"))
    return jax.shard_map(
        on_device, mesh=mesh, in_specs=in_specs, out_specs=out_specs, check_vma=False
    )
```

```python
import jax
import jax.numpy as jnp
from jax import lax
from jax.experimental import pallas as pl
from jax.experimental.pallas import tpu as pltpu
from jax.sharding import PartitionSpec as P

EPSILON = 1e-05
F32, BF16 = jnp.float32, jnp.bfloat16
NT = (((1,), (1,)), ((), ()))
TN = (((0,), (0,)), ((), ()))
SCOPED = 14 << 20
SMEM = pl.BlockSpec(memory_space=pltpu.SMEM)
VMEM = pl.BlockSpec(memory_space=pltpu.VMEM)
ANY = pl.BlockSpec(memory_space=pl.ANY)
HEAD = 128
COST = pl.CostEstimate(flops=8 * 10**9, bytes_accessed=10**8, transcendentals=0)
LIGHT = pl.CostEstimate(flops=1, bytes_accessed=1, transcendentals=0)


def call(body, outs, operands, first_spec=VMEM, light=False):
    return pl.pallas_call(
        body,
        in_specs=[first_spec] + [VMEM] * (len(operands) - 1),
        out_specs=[VMEM] * len(outs),
        out_shape=outs,
        compiler_params=pltpu.CompilerParams(vmem_limit_bytes=SCOPED),
        cost_estimate=LIGHT if light else COST,
    )(*operands)


def shape(dims, dtype):
    return jax.ShapeDtypeStruct(tuple(dims), dtype)


def after(array, *earlier):
    return lax.optimization_barrier((array, *earlier))[0]


def half_start(extent, other, offset):
    core = lax.axis_index("dp") % 2
    core = 1 - core if other else core
    return pl.multiple_of(core * (extent // 2) + offset, HEAD)


def grad_mixed_part(pieces, w_output, other, offset, size, received=None):
    counts = [len(p) for p in pieces]
    flat = [a for p in pieces for a in p]
    rows = sum(p[0].shape[0] for p in pieces)

    def body(*refs):
        blocks, at = [], 0
        for n in counts:
            blocks.append(jnp.concatenate([r[...] for r in refs[at : at + n]], axis=1))
            at += n
        ups = jnp.concatenate(blocks, axis=0)
        w = refs[at]
        start = half_start(w_output.shape[0], other, offset)
        part = lax.dot_general(ups, w[pl.ds(start, size), :], NT, preferred_element_type=F32)
        if other:
            refs[at + 1][...] = part.astype(BF16)
        else:
            part = part + refs[at + 1][...].astype(F32)
            refs[at + 2][...] = part
            refs[at + 3][...] = part.astype(BF16)

    if other:
        return call(body, [shape((rows, size), BF16)], [*flat, w_output])
    outs = [shape((rows, size), F32), shape((rows, size), BF16)]
    return call(body, outs, [*flat, w_output, received])


def unmix(kept, received, mixing, first_head):
    rows, size = kept.shape
    count = len(received)

    def body(*refs):
        mix, out = refs[count + 1], refs[count + 2]
        for h in range(size // HEAD):
            cols = slice(h * HEAD, (h + 1) * HEAD)
            total = refs[0][:, cols]
            for r in refs[1 : count + 1]:
                total = total + r[:, cols].astype(F32)
            out[:, cols] = lax.dot_general(
                mix[first_head + h], total.astype(BF16), TN, preferred_element_type=F32
            ).astype(BF16)

    return call(body, [shape((rows, size), BF16)], [kept, *received, mixing])


def grad_normed_part(grads, w_value, other, offset, total=None, pieces=0, span=None):
    begin, end = span or (0, w_value.shape[0])
    (rows, size), width = grads.shape, end - begin

    def body(v, w, *refs):
        start = half_start(w_value.shape[1], other, offset)
        sums = lax.dot_general(v[...], w[begin:end, pl.ds(start, size)], NT, preferred_element_type=F32)
        if total is not None:
            sums = sums + refs[0][:, begin:end]
        if not pieces:
            refs[-1][...] = sums
            return
        keep, *sends = refs[-pieces:]
        own = rows // pieces
        keep[...] = sums[:own]
        for t, ref in enumerate(sends):
            ref[...] = sums[(t + 1) * own : (t + 2) * own].astype(BF16)

    if pieces:
        outs = [shape((rows // pieces, width), F32)] + [shape((rows // pieces, width), BF16)] * (pieces - 1)
    else:
        outs = [shape((rows, width), F32)]
    operands = [grads, pltpu.with_memory_space_constraint(w_value, pltpu.VMEM)] + ([] if total is None else [total])
    return call(body, outs, operands)


def stacked(columns):
    rows = columns[0].shape[0]
    lane = lax.broadcasted_iota(jnp.int32, (rows, 128), 1)
    wide = jnp.zeros((rows, 128), F32)
    for k, column in enumerate(columns):
        wide = jnp.where(lane == k, column, wide)
    if rows % 128:
        wide = jnp.concatenate([wide, jnp.zeros((-rows % 128, 128), F32)], axis=0)
    return wide.T[:8]


def as_columns(stats, rows):
    return jnp.concatenate([stats, jnp.zeros((120, stats.shape[1]), F32)], axis=0).T[:rows]


def ordered(store, table):
    slots = store.shape[0]

    def body(s, store_ref, *outs):
        section = lax.axis_index("section")
        for k, out in enumerate(outs):
            out[...] = store_ref[s[k, section]]

    return call(body, [shape(store.shape[1:], BF16)] * slots, [table, store], SMEM, light=True)


def width_sums(keep, received, inputs, slot):
    own, width = keep[0].shape[0], sum(k.shape[1] for k in keep)
    count = len(keep)
    slots = len(inputs)

    def body(*refs):
        keeps, refs = refs[:count], refs[count:]
        ins, refs = refs[:slots], refs[slots:]
        grad_ref, stats = refs[-2:]
        parts = []
        for k, ref in enumerate(keeps):
            part = ref[...]
            for r in refs[k:-2:count]:
                part = part + r[...].astype(F32)
            parts.append(part)
        grad = jnp.concatenate(parts, axis=1)
        grad_ref[...] = grad
        floats = [r[...].astype(F32) for r in ins]
        columns = [jnp.sum(grad, axis=1, keepdims=True), jnp.sum(grad * floats[slot], axis=1, keepdims=True)]
        if slot == 0:
            for x in floats:
                columns += [jnp.sum(x, axis=1, keepdims=True), jnp.sum(x * x, axis=1, keepdims=True)]
        stats[...] = stacked(columns)

    outs = [shape((own, width), F32), shape((8, -(-own // 128) * 128), F32)]
    return call(body, outs, [*keep, *inputs, *received])


def finish(grad, upstream, inputs, slot, input_stats, grad_stats, width, parts):
    own, part = grad.shape
    slots = len(inputs)
    n_up, n_in, n_grad = len(upstream), len(input_stats), len(grad_stats)

    def body(grad_ref, *refs):
        x_refs, refs = refs[:slots], refs[slots:]
        ups, refs = refs[:n_up], refs[n_up:]
        ins, refs = refs[:n_in], refs[n_in:]
        grads, outs = refs[:n_grad], refs[n_grad:]
        total_in = ins[0][...]
        for r in ins[1:]:
            total_in = total_in + r[...]
        total = grads[0][...]
        for r in grads[1:]:
            total = total + r[...]
        in_columns = as_columns(total_in, own)
        columns = as_columns(total, own)

        def normal(k):
            center = in_columns[:, 2 * k + 2 : 2 * k + 3] / width
            inverse = lax.rsqrt(in_columns[:, 2 * k + 3 : 2 * k + 4] / width - center * center + EPSILON)
            return center, inverse, (x_refs[k][...].astype(F32) - center) * inverse

        center, inverse, scaled = normal(slot)
        first = columns[:, 0:1]
        second = (columns[:, 1:2] - center * first) * inverse
        above = jnp.concatenate([r[...] for r in ups], axis=1).astype(F32)
        made = (above + inverse * (grad_ref[...] - first / width - scaled * (second / width))).astype(BF16)
        for k in range(parts):
            outs[k][...] = made[:, k * (part // parts) : (k + 1) * (part // parts)]
        if slot == 0:
            for k in range(slots):
                outs[parts + k][...] = (scaled if k == slot else normal(k)[2]).astype(BF16)

    operands = [grad, *inputs, *upstream, *input_stats, *grad_stats]
    outs = [shape((own, part // parts), BF16)] * parts
    if slot == 0:
        outs += [shape((own, part), BF16)] * slots
    return call(body, outs, operands)


def value_grad(normed, terms, dims):
    depth, width = sum(a.shape[0] for a in normed), normed[0].shape[1]
    blocks, count = len(normed), len(terms)
    slots, size = len(terms[0][0]), terms[0][0][0].shape[1]
    block = 256 if width % 256 == 0 else 128
    steps = width // block

    def body(*refs):
        norms, refs = refs[:blocks], refs[blocks:]
        grads, refs = refs[: count * slots], refs[count * slots :]
        out, made, sems = refs
        copies = []
        for k, (_, other, offset) in enumerate(terms):
            v = jnp.concatenate([r[...] for r in grads[k * slots : (k + 1) * slots]], axis=0)
            start = half_start(dims[1], other, offset)
            for i in range(steps):
                rows = pl.ds(i * block, block)
                made[k, rows, :] = lax.dot_general(
                    jnp.concatenate([n[:, i * block : (i + 1) * block] for n in norms], axis=0),
                    v,
                    TN,
                    preferred_element_type=F32,
                ).astype(BF16)
                copies.append(
                    pltpu.make_async_copy(
                        made.at[k, rows], out.at[rows, pl.ds(start, size)], sems.at[k, i]
                    )
                )
                copies[-1].start()
        for copy in copies:
            copy.wait()

    flat = [g for grads, _, _ in terms for g in grads]
    return pl.pallas_call(
        body,
        in_specs=[VMEM] * (blocks + len(flat)),
        out_specs=[ANY],
        out_shape=[pltpu.HBM(dims, BF16)],
        scratch_shapes=[pltpu.VMEM((count, width, size), BF16), pltpu.SemaphoreType.DMA((count, steps))],
        compiler_params=pltpu.CompilerParams(vmem_limit_bytes=SCOPED),
        cost_estimate=COST,
    )(*normed, *flat)


def mixing_weights(slopes, length, own):
    heads = slopes.shape[1] // 2

    def body(slopes_ref, out):
        tensor = lax.axis_index("tensor")
        first = (lax.axis_index("dp") % 2) * heads

        def place(dim):
            local = lax.broadcasted_iota(jnp.int32, (length, length), dim)
            return ((local // own) ^ tensor) * own + local % own

        distance = (place(0) - place(1)).astype(F32)
        causal = distance >= 0
        distance = jnp.where(causal, distance, 0.0)
        lane = lax.broadcasted_iota(jnp.int32, slopes.shape, 1)
        for h in range(heads):
            slope = jnp.sum(jnp.where(lane == first + h, slopes_ref[...], 0.0), axis=1, keepdims=True)
            weights = jnp.where(causal, jnp.exp(-slope * distance), 0.0)
            out[h] = (weights / jnp.sum(weights, axis=-1, keepdims=True)).astype(BF16)

    return call(body, [shape((heads, length, length), BF16)], [slopes])


def flipped(array, axis, mask):
    return lax.ppermute(array, axis, [(i, i ^ mask) for i in range(lax.axis_size(axis))])


def on_device(parked, arriving, slot_table, value_weight, output_weight, slopes):
    sections, tensors, parts = (lax.axis_size(a) for a in ("section", "tensor", "dp"))
    slots, own, part_width = parked.shape[1:]
    width = part_width * parts
    half = output_weight.shape[1] // 2
    others = range(1, tensors)
    chips = range(2, parts, 2)
    bounds = [0, half // 2, half]
    chunks = [(a, b - a) for a, b in zip(bounds[:-1], bounds[1:], strict=True)]
    final = len(chunks) - 1

    def others_of(array):
        return [flipped(array, "tensor", t) for t in others]

    token = [None]

    def run(kernel, first, *rest):
        if token[0] is not None:
            if isinstance(first, list):
                first = [after(first[0], token[0]), *first[1:]]
            else:
                first = after(first, token[0])
        outs = kernel(first, *rest)
        token[0] = outs[0]
        return outs

    upstream = [arriving[0]]
    pieces = [[a] for a in [upstream[0], *others_of(upstream[0])]]
    mixing, = run(mixing_weights, slopes[None], own * tensors, own)
    pieces[0][0] = after(pieces[0][0], mixing)
    w_output = pltpu.with_memory_space_constraint(output_weight[0], pltpu.VMEM)
    values = []
    for slot in range(slots):
        last = slot == slots - 1
        if slot > 0:
            def from_above(array, t):
                return lax.ppermute(
                    array,
                    ("section", "tensor"),
                    [(i * tensors + k, (i - 1) * tensors + (k ^ t)) for i in range(1, sections) for k in range(tensors)],
                )

            above, upstream = upstream, [from_above(a, 0) for a in upstream]
            pieces = [upstream] + [[from_above(above[0], t), *(flipped(a, "tensor", t) for a in upstream[1:])] for t in others]

        def product(j, other, received=None):
            a, n = chunks[j]
            mixed = lambda first, *rest: grad_mixed_part([first, *pieces[1:]], *rest)
            return run(mixed, pieces[0], w_output, other, a, n, received)

        halves, kept, across = [], [], []
        for j in range(len(chunks) + 1):
            if j <= final:
                halves.append(flipped(product(j, True)[0], "dp", 1))
            if j > 0:
                outs = product(j - 1, False, halves[j - 1])
                kept.append(outs[:2])
                if last and j == len(chunks):
                    normed = [after(a, outs[0]) for a in normed]
                    blocks = [b for a in normed for b in [a, *others_of(a)]]
                across.append([flipped(outs[1], "dp", m) for m in chips])
        if slot == 0:
            store = lax.ppermute(
                after(parked[0], kept[-1][1]), "section", [(i, sections - 1 - i) for i in range(sections)]
            )
        mine, theirs, total = [], [], None
        for j, (a, n) in enumerate(chunks):
            mine += run(unmix, kept[j][0], across[j], mixing, a // HEAD)
            theirs.append(flipped(mine[j], "dp", 1))
            for side, grads in enumerate((mine[j], theirs[j])):
                end = j == final and side == 1
                if not end:
                    total, = run(grad_normed_part, grads, value_weight[0], side == 1, a, total)
        keep, sends = [], []
        middle = part_width if last else part_width // 2
        for span in ((0, middle), (middle, part_width))[: 1 if last else 2]:
            kept_part, *sent = run(
                grad_normed_part, theirs[-1], value_weight[0], True, chunks[-1][0], total, tensors, span
            )
            keep.append(kept_part)
            sends.append(sent)
        values.append([mine, theirs])
        received = [flipped(sent[t - 1], "tensor", t) for t in others for sent in sends]
        if slot == 0:
            inputs = run(ordered, store, slot_table.T)
        if last:
            terms = [
                ([v[side][j] for v in values], side == 1, a) for j, (a, _) in enumerate(chunks) for side in range(2)
            ]
            result, = run(value_grad, blocks, terms, value_weight.shape[1:])
        grad, sums = run(width_sums, keep, received, inputs, slot)
        grad_stats = [sums] + [flipped(sums, "dp", m) for m in range(1, parts)]
        if slot == 0:
            input_stats = grad_stats
        outs = run(finish, grad, upstream, inputs, slot, input_stats, grad_stats, width, 1 if last else 2)
        if slot == 0:
            normed = outs[-slots:]
            outs = outs[:-slots]
        upstream = outs

    return (upstream[0][None], result[None])


def solution(mesh):
    in_specs = (
        P("section", None, "tensor", "dp"),
        P("section", "tensor", "dp"),
        P(),
        P("section", "dp", "tensor"),
        P("section", "tensor", "dp"),
        P("tensor"),
    )
    out_specs = (P("section", "tensor", "dp"), P("section", "dp", "tensor"))
    return jax.shard_map(
        on_device, mesh=mesh, in_specs=in_specs, out_specs=out_specs, check_vma=False
    )
```
